32 devices in a mesh: facet: 4 (over y, core), base: 8 (over z, x).
Axes of the slice: x: 2, y: 2, z: 4, core: 2. Of those that a mesh axis runs over, the one named last changes fastest.
Arguments:
- facets: bfloat16 [64, 16, 2, 4096], P('base', 'facet'), may hold values from -6 to 6
- observed: bfloat16 [64, 2, 1024], P('base'), may hold values from -6 to 6
- sub_u: int32 [64], P('base'), may hold values from -16384 to 16352
- sub_v: int32 [64], P('base'), may hold values from -16384 to 16352
- sub_block: int32 [64], P('base'), may hold values from 0 to 127
- sub_count: int32 [64], P('base'), may hold values from 0 to 4096, as said below
- gain_real: float32 [128], replicated, may hold values from 0.5 to 1.5
- gain_imag: float32 [128], replicated, may hold values from -0.5 to 0.5
Outputs:
- facet_residual: float32 [64, 16, 2, 4096], P('base', 'facet')
- residual_grids: bfloat16 [64, 2, 1024], P('base')
The draws below stay inside these ranges and needn't reach their ends.
Inputs may be any that keep to these rules, and one draw needn't show every extreme that they name: `sub_count`: each slot holds a subgrid with that many visibilities, 0 for an empty slot; some slot holds 4096.
All inputs are finite; a program needn't handle non-finite values.
Results may differ from the reference program's by a relative error of at most 0.0053.
Values may be sent and summed in bfloat16 or wider, within the bound.
A program may use at most 256 MiB of HBM per device.

```python
import math
import jax
import jax.numpy as jnp
from jax import lax

FS = 4096
NPIX = 32768
SG = 32
NF = 16
STRIP_ROWS = 64
SUBS = 8
NSUB = 64
BLOCKS = 128
CMAX = 4096


def draw_sub_count(key, part):
    key_live, key_count = jax.random.split(key)
    shard_index = jnp.arange(NSUB, dtype=jnp.int32) // SUBS
    shards = NSUB // SUBS
    ticket = jax.random.randint(key_live, (NSUB,), 0, 100 * shards, dtype=jnp.int32)
    is_live = ticket < 25 * shards + 70 * shard_index
    visits = jax.random.randint(key_count, (NSUB,), 1, CMAX + 1, dtype=jnp.int32)
    counts_drawn = jnp.where(is_live, visits, 0)
    return counts_drawn.at[0].set(CMAX)


def touch_ends(array, key, low, largest):
    index_at = [jax.random.randint(jax.random.fold_in(key, axis), (), 0, length) for axis, length in enumerate(array.shape)]
    main_axis = array.shape.index(max(array.shape))
    beside = index_at[:main_axis] + [(index_at[main_axis] + 1) % array.shape[main_axis]] + index_at[main_axis + 1:]
    return array.at[tuple(index_at)].set(low).at[tuple(beside)].set(largest)


def shard_levels(key, extent, pieces, low, top_value):
    def one(position, blocks):
        draws = jax.random.uniform(jax.random.fold_in(jax.random.fold_in(key, 6), position), (blocks,), jnp.float32, low / len(pieces), top_value / len(pieces))
        return jnp.repeat(jnp.exp(draws), extent[position] // blocks).reshape((-1,) + (1,) * (len(extent) - position - 1))

    gain = one(*pieces[0])
    for cut in pieces[1:]:
        gain = gain * one(*cut)
    return gain


def centred(stream_key, shape, deviation, limit, cuts=(), held_as=jnp.bfloat16):
    loudness = shard_levels(stream_key, shape, cuts, -0.22, 0.18) if cuts else 1.0
    entries = jax.random.normal(stream_key, shape, jnp.float32) * deviation * loudness
    return jnp.minimum(jnp.maximum(entries, -limit), limit).astype(held_as)


def setup_inputs(seed: int = 0) -> dict:
    splits = jax.random.split(jax.random.key(seed), 9)
    facets = centred(splits[0], (STRIP_ROWS, NF, 2, FS), 1.0, 6.0, ((0, 8), (1, 4)))
    observed = centred(splits[1], (NSUB, 2, SG * SG), 1.0, 6.0, ((0, 8),))
    sub_u = touch_ends(jax.random.randint(splits[2], (NSUB,), 0 - NPIX // 2, NPIX // 2 - SG + 1), jax.random.fold_in(splits[2], 1), 0 - NPIX // 2, (NPIX // 2 - SG + 1) - 1).astype(jnp.int32)
    sub_v = touch_ends(jax.random.randint(splits[3], (NSUB,), 0 - NPIX // 2, NPIX // 2 - SG + 1), jax.random.fold_in(splits[3], 1), 0 - NPIX // 2, (NPIX // 2 - SG + 1) - 1).astype(jnp.int32)
    sub_block = touch_ends(jax.random.randint(splits[4], (NSUB,), 0, BLOCKS), jax.random.fold_in(splits[4], 1), 0, BLOCKS - 1).astype(jnp.int32)
    sub_count = draw_sub_count(jax.random.fold_in(splits[8], 71), 0)
    gain_real = jnp.clip(1.0 + 0.1 * jax.random.normal(splits[6], (BLOCKS,), jnp.float32), 0.5, 1.5)
    gain_imag = jnp.clip(jax.random.uniform(splits[7], (BLOCKS,), jnp.float32, -0.5, 0.5), -0.5, 0.5)
    return {"facets": facets, "observed": observed, "sub_u": sub_u, "sub_v": sub_v, "sub_block": sub_block, "sub_count": sub_count, "gain_real": gain_real, "gain_imag": gain_imag}


def column_tables(facet_id, v_list):
    column_place = (facet_id % 4 + 2) * FS + jnp.arange(FS, dtype=jnp.int32)
    frequency = (v_list[:, None] + jnp.arange(SG, dtype=jnp.int32)[None, :]).reshape(-1)
    cycles = jnp.mod(column_place[:, None] * frequency[None, :], NPIX)
    phases = cycles.astype(jnp.float32) * (2.0 * math.pi / NPIX)
    return (jnp.cos(phases).astype(jnp.bfloat16), jnp.sin(phases).astype(jnp.bfloat16))

def strip_rows(facet_id, first_row, row_count, total_rows):
    return (facet_id // 4 + 2) * FS + (FS - total_rows) // 2 + first_row + jnp.arange(row_count, dtype=jnp.int32)

def row_tables(u_list, row_place):
    frequency = u_list[:, None] + jnp.arange(SG, dtype=jnp.int32)[None, :]
    cycles = jnp.mod(frequency[:, :, None] * row_place[None, None, :], NPIX)
    phases = cycles.astype(jnp.float32) * (2.0 * math.pi / NPIX)
    return (jnp.cos(phases).astype(jnp.bfloat16), jnp.sin(phases).astype(jnp.bfloat16))

def along_columns(left, table):
    return lax.dot_general(left, table, (((1,), (1,)), ((), ())), preferred_element_type=jnp.float32)

def batched(form, left, right):
    return jnp.einsum(form, left.astype(jnp.float32), right.astype(jnp.float32), precision=lax.Precision.HIGHEST)

def degrid_piece(block_rows, col_cos, col_sin, row_cos, row_sin):
    row_count = block_rows.shape[0]
    slots = row_cos.shape[0]
    real_rows = block_rows[:, 0, :]
    imag_rows = block_rows[:, 1, :]
    strip_real = jnp.dot(real_rows, col_cos, preferred_element_type=jnp.float32) + jnp.dot(imag_rows, col_sin, preferred_element_type=jnp.float32)
    strip_imag = jnp.dot(imag_rows, col_cos, preferred_element_type=jnp.float32) - jnp.dot(real_rows, col_sin, preferred_element_type=jnp.float32)
    strip_real = strip_real.astype(jnp.bfloat16).reshape(row_count, slots, SG)
    strip_imag = strip_imag.astype(jnp.bfloat16).reshape(row_count, slots, SG)
    model_real = batched('npk,knq->npq', row_cos, strip_real) + batched('npk,knq->npq', row_sin, strip_imag)
    model_imag = batched('npk,knq->npq', row_cos, strip_imag) - batched('npk,knq->npq', row_sin, strip_real)
    return jnp.stack([model_real, model_imag], 1).reshape(slots, 2, SG * SG)

def grid_piece(residual_block, col_cos, col_sin, row_cos, row_sin):
    slots = residual_block.shape[0]
    row_count = row_cos.shape[2]
    cells = residual_block.reshape(slots, 2, SG, SG)
    cell_real = cells[:, 0]
    cell_imag = cells[:, 1]
    lift_real = batched('npk,npq->knq', row_cos, cell_real) - batched('npk,npq->knq', row_sin, cell_imag)
    lift_imag = batched('npk,npq->knq', row_cos, cell_imag) + batched('npk,npq->knq', row_sin, cell_real)
    lift_real = lift_real.reshape(row_count, slots * SG).astype(jnp.bfloat16)
    lift_imag = lift_imag.reshape(row_count, slots * SG).astype(jnp.bfloat16)
    grid_real = along_columns(lift_real, col_cos) - along_columns(lift_imag, col_sin)
    grid_imag = along_columns(lift_real, col_sin) + along_columns(lift_imag, col_cos)
    return jnp.stack([grid_real, grid_imag], 1)

def weighted_residual(model, observed, sub_block, sub_count, gain_real, gain_imag):
    block_hits = sub_block[:, None] == jnp.arange(BLOCKS, dtype=jnp.int32)[None, :]
    gain_re_rows = lax.optimization_barrier(jnp.sum(jnp.where(block_hits, gain_real[None, :], 0.0), axis=1))[:, None]
    gain_im_rows = lax.optimization_barrier(jnp.sum(jnp.where(block_hits, gain_imag[None, :], 0.0), axis=1))[:, None]
    weight = (sub_count.astype(jnp.float32) / CMAX)[:, None]
    seen = observed.astype(jnp.float32)
    model_real = model[:, 0]
    model_imag = model[:, 1]
    diff_real = seen[:, 0] - (gain_re_rows * model_real - gain_im_rows * model_imag)
    diff_imag = seen[:, 1] - (gain_re_rows * model_imag + gain_im_rows * model_real)
    out_real = weight * (gain_re_rows * diff_real + gain_im_rows * diff_imag)
    out_imag = weight * (gain_re_rows * diff_imag - gain_im_rows * diff_real)
    return jnp.stack([out_real, out_imag], 1).astype(jnp.bfloat16)

def reference(facets, observed, sub_u, sub_v, sub_block, sub_count, gain_real, gain_imag):
    total_rows = facets.shape[0]
    blocks_count = NSUB // SUBS
    norm_scale = 1.0 / math.sqrt(NF * total_rows * FS)
    u_blocks = sub_u.reshape(blocks_count, SUBS)
    v_blocks = sub_v.reshape(blocks_count, SUBS)
    facet_list = jnp.arange(NF, dtype=jnp.int32)

    def degrid_block(offsets):
        u_list, v_list = offsets

        def one_facet(summed, facet_id):
            strip = lax.dynamic_index_in_dim(facets, facet_id, 1, keepdims=False)
            col_cos, col_sin = column_tables(facet_id, v_list)
            row_cos, row_sin = row_tables(u_list, strip_rows(facet_id, 0, total_rows, total_rows))
            return (summed + degrid_piece(strip, col_cos, col_sin, row_cos, row_sin), None)
        summed, unused = lax.scan(one_facet, jnp.zeros((SUBS, 2, SG * SG), jnp.float32), facet_list)
        return summed
    model = lax.map(degrid_block, (u_blocks, v_blocks)).reshape(NSUB, 2, SG * SG) * norm_scale
    residual = weighted_residual(model, observed, sub_block, sub_count, gain_real, gain_imag)
    residual_blocks = residual.reshape(blocks_count, SUBS, 2, SG * SG)

    def grid_facet(facet_id):

        def one_block(summed, block_data):
            u_list, v_list, residual_block = block_data
            col_cos, col_sin = column_tables(facet_id, v_list)
            row_cos, row_sin = row_tables(u_list, strip_rows(facet_id, 0, total_rows, total_rows))
            return (summed + grid_piece(residual_block, col_cos, col_sin, row_cos, row_sin), None)
        summed, unused = lax.scan(one_block, jnp.zeros((total_rows, 2, FS), jnp.float32), (u_blocks, v_blocks, residual_blocks))
        return summed
    gridded = lax.map(grid_facet, facet_list)
    facet_residual = jnp.transpose(gridded, (1, 0, 2, 3)) * norm_scale
    return (facet_residual, residual)
```

```python
import functools
import math

import jax
import jax.numpy as jnp
from jax import lax
from jax.experimental import pallas as pl
from jax.experimental.pallas import tpu as pltpu
from jax.sharding import PartitionSpec as P

FS = 4096
NPIX = 32768
SG = 32
NF = 16
CMAX = 4096
QUARTER = NPIX // 4
MESH = pl.DeviceIdType.MESH

LOW = 256
HIGH = FS // LOW
COLS = 4
ROWS = 8
SLOTS = 8
LANES = SLOTS * SG
STEP = 16


def cos_turns(turns):
    away = jnp.abs(((turns + NPIX // 2) & (NPIX - 1)) - NPIX // 2)
    x = (QUARTER - away).astype(jnp.float32) * (2.0 * math.pi / NPIX)
    x2 = x * x
    tail = -1.0 / 39916800
    for term in (362880, -5040, 120, -6):
        tail = tail * x2 + 1.0 / term
    return x + x * (x2 * tail)


def iota(shape, dim):
    return lax.broadcasted_iota(jnp.int32, shape, dim)


def per_lane(values, shape):
    owner = iota(shape, len(shape) - 1) // SG
    out = jnp.full(shape, values[0])
    for s in range(1, SLOTS):
        out = jnp.where(owner == s, values[s], out)
    return out


def kernel(
    n, nf, scale,
    v_ref, u_ref, block_ref, count_ref, gain_re_ref, gain_im_ref, seen_ref, facet_ref,
    out_ref, res_ref,
    freq, low_table, high_table, row_table, product, strip_out, strip, model, lift, lifted, spread,
    v_send, v_recv, s_send, s_recv, m_send, m_recv, l_send, l_recv,
):
    me = lax.axis_index("base")
    mf = lax.axis_index("facet")

    def on_base(k):
        return {"base": lax.rem(me + k, n)}

    def on_facet(k):
        return {"facet": lax.rem(mf + k, nf)}

    barrier = pltpu.get_barrier_semaphore()

    def greet_base(k, _):
        pl.semaphore_signal(barrier, inc=1, device_id=on_base(k), device_id_type=MESH)
        return 0

    lax.fori_loop(1, n, greet_base, 0)
    for k in range(1, nf):
        pl.semaphore_signal(barrier, inc=1, device_id=on_facet(k), device_id_type=MESH)

    own_freq = per_lane([v_ref[s] for s in range(SLOTS)], (8, LANES)) + iota((8, LANES), 1) % SG
    freq[me] = own_freq

    pl.semaphore_wait(barrier, n - 1 + nf - 1)

    def v_copy(k, slot):
        return pltpu.make_async_remote_copy(
            src_ref=freq.at[me], dst_ref=freq.at[slot], send_sem=v_send.at[k],
            recv_sem=v_recv.at[k], device_id=on_base(k), device_id_type=MESH,
        )

    def send_v(k, _):
        v_copy(k, me).start()
        return 0

    lax.fori_loop(1, n, send_v, 0)

    wide = n * 2 * ROWS
    lane = iota((2 * SG, wide), 1)
    sub = iota((2 * SG, wide), 0)
    place = (mf + 2) * FS + (FS - n * ROWS) // 2 + lane // (2 * ROWS) * ROWS + lane % ROWS
    turn = (sub // SG - lane // ROWS % 2) * QUARTER
    for s in range(SLOTS):
        row_table[pl.ds(s * 2 * SG, 2 * SG), :] = cos_turns(
            (sub % SG + u_ref[s]) * place + turn
        ).astype(jnp.bfloat16)

    def strip_copy(k, slot):
        return pltpu.make_async_remote_copy(
            src_ref=strip_out.at[k], dst_ref=strip.at[slot], send_sem=s_send.at[k],
            recv_sem=s_recv.at[k], device_id=on_base(k), device_id_type=MESH,
        )

    def degrid(k, _):
        g = lax.rem(me + k, n)

        @pl.when(k > 0)
        def _():
            v_copy(n - k, g).wait_recv()

        f = freq[g]
        line = iota((HIGH, 8, LANES), 1)
        y = (line % COLS + 2) * FS + iota((HIGH, 8, LANES), 0) * LOW
        high_table[g] = cos_turns(f[None] * y - line // COLS * QUARTER)
        fine = iota((STEP, LANES), 0)
        f2 = jnp.concatenate([f, f], 0)
        fine_cos = cos_turns(f2 * fine)
        fine_sin = cos_turns(f2 * fine - QUARTER)
        step_cos = cos_turns(f2 * fine * STEP)
        step_sin = cos_turns(f2 * fine * STEP - QUARTER)
        for i in range(LOW // STEP):
            c = step_cos[i : i + 1]
            s = step_sin[i : i + 1]
            rows = pl.ds(i * STEP, STEP)
            low_table[g, rows, 0:LANES] = (c * fine_cos - s * fine_sin).astype(jnp.bfloat16)
            low_table[g, rows, LANES : 2 * LANES] = (s * fine_cos + c * fine_sin).astype(
                jnp.bfloat16
            )
        product[...] = jnp.dot(
            facet_ref[...], low_table[g], preferred_element_type=jnp.float32
        ).reshape(HIGH, 2 * COLS * ROWS, 2 * LANES)

        def fold(h, total):
            total_re, total_im = total
            table = high_table[g, h]
            for b in range(COLS):
                re = pl.ds(b * ROWS, ROWS)
                im = pl.ds((COLS + b) * ROWS, ROWS)
                part_re = product[h, re, 0:LANES] + product[h, im, LANES : 2 * LANES]
                part_im = product[h, im, 0:LANES] - product[h, re, LANES : 2 * LANES]
                c = table[b : b + 1]
                s = table[COLS + b : COLS + b + 1]
                total_re = total_re + (part_re * c + part_im * s)
                total_im = total_im + (part_im * c - part_re * s)
            return total_re, total_im

        zero = jnp.zeros((ROWS, LANES), jnp.float32)
        total_re, total_im = lax.fori_loop(0, HIGH, fold, (zero, zero))
        chunk = jnp.concatenate([total_re, total_im], 0).astype(jnp.bfloat16)

        @pl.when(k == 0)
        def _():
            strip[me] = chunk

        @pl.when(k > 0)
        def _():
            strip_out[k] = chunk
            strip_copy(k, me).start()

        return 0

    lax.fori_loop(0, n, degrid, 0)

    def take_strip(k, _):
        strip_copy(k, lax.rem(me + n - k, n)).wait_recv()
        return 0

    lax.fori_loop(1, n, take_strip, 0)

    owner = iota((2 * SG, LANES), 1) // SG
    crossed = jnp.dot(
        row_table[...], strip[...].reshape(wide, LANES), preferred_element_type=jnp.float32
    )
    part = jnp.zeros((2 * SG, LANES), jnp.float32)
    for s in range(SLOTS):
        part = jnp.where(owner == s, crossed[s * 2 * SG : (s + 1) * 2 * SG], part)
    model[mf] = part

    def model_copy(k, slot):
        return pltpu.make_async_remote_copy(
            src_ref=model.at[mf], dst_ref=model.at[slot], send_sem=m_send.at[k],
            recv_sem=m_recv.at[k], device_id=on_facet(k), device_id_type=MESH,
        )

    for k in range(1, nf):
        model_copy(k, mf).start()

    half = (SG, LANES)
    gain_re = per_lane([gain_re_ref[block_ref[s]] for s in range(SLOTS)], half)
    gain_im = per_lane([gain_im_ref[block_ref[s]] for s in range(SLOTS)], half)
    weight = per_lane([count_ref[s] for s in range(SLOTS)], half).astype(jnp.float32) / CMAX
    seen = seen_ref[...].astype(jnp.float32)

    for k in range(1, nf):
        model_copy(k, lax.rem(mf + nf - k, nf)).wait_recv()

    whole = model[0]
    for other in range(1, nf):
        whole = whole + model[other]
    whole = whole * scale
    model_re = whole[:SG]
    model_im = whole[SG:]
    diff_re = seen[:SG] - (gain_re * model_re - gain_im * model_im)
    diff_im = seen[SG:] - (gain_re * model_im + gain_im * model_re)
    res_re = weight * (gain_re * diff_re + gain_im * diff_im)
    res_im = weight * (gain_re * diff_im - gain_im * diff_re)
    residual = jnp.concatenate([res_re, res_im], 0)
    res_ref[...] = residual.astype(jnp.bfloat16)

    blocks = jnp.concatenate(
        [jnp.where(owner == s, residual, 0.0).astype(jnp.bfloat16) for s in range(SLOTS)], 0
    )
    raised = lax.dot_general(
        row_table[...], blocks, (((0,), (0,)), ((), ())), preferred_element_type=jnp.float32
    )
    lift[...] = raised.astype(jnp.bfloat16).reshape(n, 2 * ROWS, LANES)

    def lift_copy(k, slot):
        return pltpu.make_async_remote_copy(
            src_ref=lift.at[lax.rem(me + k, n)], dst_ref=lifted.at[slot], send_sem=l_send.at[k],
            recv_sem=l_recv.at[k], device_id=on_base(k), device_id_type=MESH,
        )

    def send_lift(k, _):
        lift_copy(k, me).start()
        return 0

    lax.fori_loop(1, n, send_lift, 0)
    lifted[me] = lift[me]

    def grid(k, _):
        g = lax.rem(me + n - k, n)

        @pl.when(k > 0)
        def _():
            lift_copy(k, g).wait_recv()

        value = lifted[g].astype(jnp.float32) * scale
        value_re = value[:ROWS]
        value_im = value[ROWS:]

        def turn_one(h, _):
            table = high_table[g, h]
            re = []
            im = []
            for b in range(COLS):
                c = table[b : b + 1]
                s = table[COLS + b : COLS + b + 1]
                re.append(value_re * c - value_im * s)
                im.append(value_re * s + value_im * c)
            re = jnp.concatenate(re, 0)
            im = jnp.concatenate(im, 0)
            half_rows = COLS * ROWS
            spread[h, 0:half_rows, 0:LANES] = re.astype(jnp.bfloat16)
            spread[h, 0:half_rows, LANES : 2 * LANES] = (-im).astype(jnp.bfloat16)
            spread[h, half_rows : 2 * half_rows, 0:LANES] = im.astype(jnp.bfloat16)
            spread[h, half_rows : 2 * half_rows, LANES : 2 * LANES] = re.astype(jnp.bfloat16)
            return 0

        lax.fori_loop(0, HIGH, turn_one, 0)
        term = lax.dot_general(
            spread[...].reshape(HIGH * 2 * COLS * ROWS, 2 * LANES),
            low_table[g],
            (((1,), (1,)), ((), ())),
            preferred_element_type=jnp.float32,
        )

        @pl.when(k == 0)
        def _():
            out_ref[...] = term

        @pl.when(k > 0)
        def _():
            out_ref[...] += term

        return 0

    lax.fori_loop(0, n, grid, 0)

    def drain(k, _):
        v_copy(k, me).wait_send()
        strip_copy(k, me).wait_send()
        lift_copy(k, me).wait_send()
        return 0

    lax.fori_loop(1, n, drain, 0)
    for k in range(1, nf):
        model_copy(k, mf).wait_send()


def per_device(facets, observed, sub_u, sub_v, sub_block, sub_count, gain_real, gain_imag):
    n = lax.axis_size("base")
    nf = lax.axis_size("facet")
    assert facets.shape == (ROWS, COLS, 2, FS) and nf * COLS == NF
    assert observed.shape == (SLOTS, 2, SG * SG)
    scale = 1.0 / math.sqrt(NF * n * ROWS * FS)
    rows = facets.reshape(ROWS, COLS, 2, HIGH, LOW).transpose(3, 2, 1, 0, 4).reshape(-1, LOW)
    seen = observed.reshape(SLOTS, 2, SG, SG).transpose(1, 2, 0, 3).reshape(2 * SG, LANES)
    smem = pl.BlockSpec(memory_space=pltpu.SMEM)
    vmem = pl.BlockSpec(memory_space=pltpu.VMEM)
    bf16 = jnp.bfloat16
    f32 = jnp.float32
    dma = pltpu.SemaphoreType.DMA
    out, res = pl.pallas_call(
        functools.partial(kernel, n, nf, scale),
        out_shape=(
            jax.ShapeDtypeStruct((HIGH * 2 * COLS * ROWS, LOW), f32),
            jax.ShapeDtypeStruct((2 * SG, LANES), bf16),
        ),
        in_specs=[smem] * 6 + [vmem] * 2,
        out_specs=(vmem, vmem),
        scratch_shapes=[
            pltpu.VMEM((n, 8, LANES), jnp.int32),
            pltpu.VMEM((n, LOW, 2 * LANES), bf16),
            pltpu.VMEM((n, HIGH, 8, LANES), f32),
            pltpu.VMEM((SLOTS * 2 * SG, n * 2 * ROWS), bf16),
            pltpu.VMEM((HIGH, 2 * COLS * ROWS, 2 * LANES), f32),
            pltpu.VMEM((n, 2 * ROWS, LANES), bf16),
            pltpu.VMEM((n, 2 * ROWS, LANES), bf16),
            pltpu.VMEM((nf, 2 * SG, LANES), f32),
            pltpu.VMEM((n, 2 * ROWS, LANES), bf16),
            pltpu.VMEM((n, 2 * ROWS, LANES), bf16),
            pltpu.VMEM((HIGH, 2 * COLS * ROWS, 2 * LANES), bf16),
            dma((n,)), dma((n,)), dma((n,)), dma((n,)),
            dma((nf,)), dma((nf,)), dma((n,)), dma((n,)),
        ],
        compiler_params=pltpu.CompilerParams(
            collective_id=0, has_side_effects=True, vmem_limit_bytes=48 * 1024 * 1024
        ),
    )(sub_v, sub_u, sub_block, sub_count, gain_real, gain_imag, seen, rows)
    out = out.reshape(HIGH, 2, COLS, ROWS, LOW).transpose(3, 2, 1, 0, 4)
    res = res.reshape(2, SG, SLOTS, SG).transpose(2, 0, 1, 3)
    return (out.reshape(ROWS, COLS, 2, FS), res.reshape(SLOTS, 2, SG * SG))


def solution(mesh):
    in_specs = (
        P("base", "facet", None, None),
        P("base", None, None),
        P("base"),
        P("base"),
        P("base"),
        P("base"),
        P(),
        P(),
    )
    out_specs = (P("base", "facet", None, None), P("base", None, None))
    return jax.shard_map(
        per_device, mesh=mesh, in_specs=in_specs, out_specs=out_specs, check_vma=False
    )
```

```python
import functools
import math

import jax
import jax.numpy as jnp
from jax import lax
from jax.experimental import pallas as pl
from jax.experimental.pallas import tpu as pltpu
from jax.sharding import PartitionSpec as P

FS = 4096
NPIX = 32768
SG = 32
NF = 16
CMAX = 4096
QUARTER = NPIX // 4
MESH = pl.DeviceIdType.MESH

LOW = 512
HIGH = FS // LOW
COLS = 4
ROWS = 8
SLOTS = 8
LANES = SLOTS * SG
STEP = 16


def cos_turns(turns):
    away = jnp.abs(((turns + NPIX // 2) & (NPIX - 1)) - NPIX // 2)
    x = (QUARTER - away).astype(jnp.float32) * (2.0 * math.pi / NPIX)
    x2 = x * x
    tail = -1.0 / 39916800
    for term in (362880, -5040, 120, -6):
        tail = tail * x2 + 1.0 / term
    return x + x * (x2 * tail)


def iota(shape, dim):
    return lax.broadcasted_iota(jnp.int32, shape, dim)


def per_lane(values, shape):
    owner = iota(shape, len(shape) - 1) // SG
    out = jnp.full(shape, values[0])
    for s in range(1, SLOTS):
        out = jnp.where(owner == s, values[s], out)
    return out


def kernel(
    n, nf, scale,
    v_ref, u_ref, block_ref, count_ref, gain_re_ref, gain_im_ref, seen_ref, facet_ref,
    out_ref, res_ref,
    freq, low_table, high_one, high_two, row_table, product, strip_out, strip, lift, lifted, spread,
    v_send, v_recv, s_send, s_recv, l_send, l_recv,
):
    me = lax.axis_index("base")
    mf = lax.axis_index("facet")

    def device(k, j):
        return {"base": lax.rem(me + k, n), "facet": lax.rem(mf + j, nf)}

    barrier = pltpu.get_barrier_semaphore()

    def greet(k, _):
        for j in range(nf):
            pl.semaphore_signal(barrier, inc=1, device_id=device(k, j), device_id_type=MESH)
        return 0

    lax.fori_loop(1, n, greet, 0)
    for j in range(1, nf):
        pl.semaphore_signal(barrier, inc=1, device_id=device(0, j), device_id_type=MESH)

    freq[me] = per_lane([v_ref[s] for s in range(SLOTS)], (8, LANES)) + iota((8, LANES), 1) % SG

    wide = n * 2 * ROWS
    lane = iota((2 * SG, wide), 1)
    sub = iota((2 * SG, wide), 0)
    turn = (sub // SG - lane // ROWS % 2) * QUARTER
    first = (FS - n * ROWS) // 2 + lane // (2 * ROWS) * ROWS + lane % ROWS

    def fill_rows(s, _):
        u = sub % SG + u_ref[s]
        for a in range(nf):
            row_table[a, pl.ds(pl.multiple_of(s * 2 * SG, 2 * SG), 2 * SG), :] = cos_turns(
                u * (first + (a + 2) * FS) + turn
            ).astype(jnp.bfloat16)
        return 0

    lax.fori_loop(0, SLOTS, fill_rows, 0)

    pl.semaphore_wait(barrier, n * nf - 1)

    def v_copy(k, slot):
        return pltpu.make_async_remote_copy(
            src_ref=freq.at[me], dst_ref=freq.at[slot], send_sem=v_send.at[k],
            recv_sem=v_recv.at[k], device_id=device(k, 0), device_id_type=MESH,
        )

    def send_v(k, _):
        v_copy(k, me).start()
        return 0

    lax.fori_loop(1, n, send_v, 0)

    def strip_copy(k, j, from_facet, from_base):
        return pltpu.make_async_remote_copy(
            src_ref=strip_out.at[k], dst_ref=strip.at[from_facet, from_base],
            send_sem=s_send.at[k, j], recv_sem=s_recv.at[k, j],
            device_id=device(k, j), device_id_type=MESH,
        )

    def degrid(k, _):
        g = lax.rem(me + k, n)

        @pl.when(k > 0)
        def _():
            v_copy(n - k, g).wait_recv()

        f = freq[g]
        line = iota((8, LANES), 0)
        for h in range(HIGH):
            high = f * ((line // 2 + 2) * FS + h * LOW) - line % 2 * QUARTER
            high_one[g, h] = cos_turns(high)
            high_two[g, h] = cos_turns(high + QUARTER)
        fine = iota((STEP, LANES), 0)
        f2 = jnp.concatenate([f, f], 0)
        fine_cos = cos_turns(f2 * fine)
        fine_sin = cos_turns(f2 * fine - QUARTER)
        for i in range(LOW // STEP):
            if i % STEP == 0:
                steps = f2 * ((fine + i) * STEP)
                step_cos = cos_turns(steps)
                step_sin = cos_turns(steps - QUARTER)
            c = step_cos[i % STEP : i % STEP + 1]
            s = step_sin[i % STEP : i % STEP + 1]
            rows = pl.ds(i * STEP, STEP)
            low_table[g, rows, 0:LANES] = (c * fine_cos - s * fine_sin).astype(jnp.bfloat16)
            low_table[g, rows, LANES : 2 * LANES] = (s * fine_cos + c * fine_sin).astype(
                jnp.bfloat16
            )
        tall = jnp.concatenate([facet_ref[:, h * LOW : (h + 1) * LOW] for h in range(HIGH)], 0)
        product[...] = jnp.dot(tall, low_table[g], preferred_element_type=jnp.float32)
        lines_re = []
        lines_im = []
        for r in range(ROWS):
            total_re = jnp.zeros((8, LANES), jnp.float32)
            total_im = jnp.zeros((8, LANES), jnp.float32)
            for h in range(HIGH):
                rows = pl.ds((h * ROWS + r) * 8, 8)
                part_cos = product[rows, 0:LANES]
                part_sin = product[rows, LANES : 2 * LANES]
                one = high_one[g, h]
                two = high_two[g, h]
                total_re = total_re + (part_cos * one + part_sin * two)
                total_im = total_im + (part_cos * two - part_sin * one)
            lines_re.append(jnp.sum(total_re, 0, keepdims=True))
            lines_im.append(jnp.sum(total_im, 0, keepdims=True))
        chunk = jnp.concatenate(lines_re + lines_im, 0).astype(jnp.bfloat16)
        strip_out[k] = chunk

        @pl.when(k == 0)
        def _():
            strip[mf, me] = chunk

        @pl.when(k > 0)
        def _():
            strip_copy(k, 0, mf, me).start()

        for j in range(1, nf):
            strip_copy(k, j, mf, me).start()
        return 0

    lax.fori_loop(0, n, degrid, 0)

    half = (SG, LANES)
    gain_re = per_lane([gain_re_ref[block_ref[s]] for s in range(SLOTS)], half)
    gain_im = per_lane([gain_im_ref[block_ref[s]] for s in range(SLOTS)], half)
    weight = per_lane([count_ref[s] for s in range(SLOTS)], half).astype(jnp.float32) / CMAX
    seen = seen_ref[...].astype(jnp.float32)

    def take_strip(k, j):
        strip_copy(k, j, lax.rem(mf + nf - j, nf), lax.rem(me + n - k, n)).wait_recv()

    def take_strips(k, _):
        for j in range(nf):
            take_strip(k, j)
        return 0

    for j in range(1, nf):
        take_strip(0, j)
    lax.fori_loop(1, n, take_strips, 0)

    owner = iota((2 * SG, LANES), 1) // SG
    crossed = jnp.zeros((SLOTS * 2 * SG, LANES), jnp.float32)
    for a in range(nf):
        crossed = crossed + jnp.dot(
            row_table[a], strip[a].reshape(wide, LANES), preferred_element_type=jnp.float32
        )
    whole = jnp.zeros((2 * SG, LANES), jnp.float32)
    for s in range(SLOTS):
        whole = jnp.where(owner == s, crossed[s * 2 * SG : (s + 1) * 2 * SG], whole)
    whole = whole * scale
    model_re = whole[:SG]
    model_im = whole[SG:]
    diff_re = seen[:SG] - (gain_re * model_re - gain_im * model_im)
    diff_im = seen[SG:] - (gain_re * model_im + gain_im * model_re)
    res_re = weight * (gain_re * diff_re + gain_im * diff_im)
    res_im = weight * (gain_re * diff_im - gain_im * diff_re)
    residual = jnp.concatenate([res_re, res_im], 0)
    res_ref[...] = residual.astype(jnp.bfloat16)

    blocks = jnp.concatenate(
        [jnp.where(owner == s, residual, 0.0).astype(jnp.bfloat16) for s in range(SLOTS)], 0
    )
    raised = lax.dot_general(
        row_table[mf], blocks, (((0,), (0,)), ((), ())), preferred_element_type=jnp.float32
    )
    lift[...] = raised.astype(jnp.bfloat16).reshape(n, 2 * ROWS, LANES)

    def lift_copy(k, slot):
        return pltpu.make_async_remote_copy(
            src_ref=lift.at[lax.rem(me + k, n)], dst_ref=lifted.at[slot], send_sem=l_send.at[k],
            recv_sem=l_recv.at[k], device_id=device(k, 0), device_id_type=MESH,
        )

    def send_lift(k, _):
        lift_copy(k, me).start()
        return 0

    lax.fori_loop(1, n, send_lift, 0)
    lifted[me] = lift[me]

    def grid(k, _):
        g = lax.rem(me + n - k, n)

        @pl.when(k > 0)
        def _():
            lift_copy(k, g).wait_recv()

        value = lifted[g].astype(jnp.float32) * scale
        for h in range(HIGH):
            one = high_one[g, h]
            two = high_two[g, h]
            for r in range(0, ROWS, 2):
                by_cos = []
                by_sin = []
                for t in (r, r + 1):
                    re = value[t : t + 1]
                    im = value[ROWS + t : ROWS + t + 1]
                    by_cos.append(re * one + im * two)
                    by_sin.append(re * two - im * one)
                rows = pl.ds((h * ROWS + r) * 8, 16)
                spread[rows, 0:LANES] = jnp.concatenate(by_cos, 0).astype(jnp.bfloat16)
                spread[rows, LANES : 2 * LANES] = jnp.concatenate(by_sin, 0).astype(jnp.bfloat16)
        term = lax.dot_general(
            spread[...], low_table[g], (((1,), (1,)), ((), ())), preferred_element_type=jnp.float32
        )

        def lay(add):
            for h in range(HIGH):
                part = term[h * 8 * ROWS : (h + 1) * 8 * ROWS]
                at = pl.ds(h * LOW, LOW)
                out_ref[:, at] = out_ref[:, at] + part if add else part

        @pl.when(k == 0)
        def _():
            lay(False)

        @pl.when(k > 0)
        def _():
            lay(True)

        return 0

    lax.fori_loop(0, n, grid, 0)

    def drain(k, _):
        v_copy(k, me).wait_send()
        lift_copy(k, me).wait_send()
        for j in range(nf):
            strip_copy(k, j, mf, me).wait_send()
        return 0

    lax.fori_loop(1, n, drain, 0)
    for j in range(1, nf):
        strip_copy(0, j, mf, me).wait_send()


def per_device(facets, observed, sub_u, sub_v, sub_block, sub_count, gain_real, gain_imag):
    n = lax.axis_size("base")
    nf = lax.axis_size("facet")
    assert facets.shape == (ROWS, COLS, 2, FS) and nf * COLS == NF
    assert observed.shape == (SLOTS, 2, SG * SG)
    scale = 1.0 / math.sqrt(NF * n * ROWS * FS)
    rows = facets.reshape(ROWS * COLS * 2, FS)
    seen = observed.reshape(SLOTS, 2, SG, SG).transpose(1, 2, 0, 3).reshape(2 * SG, LANES)
    smem = pl.BlockSpec(memory_space=pltpu.SMEM)
    vmem = pl.BlockSpec(memory_space=pltpu.VMEM)
    bf16 = jnp.bfloat16
    f32 = jnp.float32
    dma = pltpu.SemaphoreType.DMA
    out, res = pl.pallas_call(
        functools.partial(kernel, n, nf, scale),
        out_shape=(
            jax.ShapeDtypeStruct((ROWS * COLS * 2, FS), f32),
            jax.ShapeDtypeStruct((2 * SG, LANES), bf16),
        ),
        in_specs=[smem] * 6 + [vmem] * 2,
        out_specs=(vmem, vmem),
        scratch_shapes=[
            pltpu.VMEM((n, 8, LANES), jnp.int32),
            pltpu.VMEM((n, LOW, 2 * LANES), bf16),
            pltpu.VMEM((n, HIGH, 8, LANES), f32),
            pltpu.VMEM((n, HIGH, 8, LANES), f32),
            pltpu.VMEM((nf, SLOTS * 2 * SG, n * 2 * ROWS), bf16),
            pltpu.VMEM((HIGH * ROWS * 8, 2 * LANES), f32),
            pltpu.VMEM((n, 2 * ROWS, LANES), bf16),
            pltpu.VMEM((nf, n, 2 * ROWS, LANES), bf16),
            pltpu.VMEM((n, 2 * ROWS, LANES), bf16),
            pltpu.VMEM((n, 2 * ROWS, LANES), bf16),
            pltpu.VMEM((HIGH * ROWS * 8, 2 * LANES), bf16),
            dma((n,)), dma((n,)), dma((n, nf)), dma((n, nf)), dma((n,)), dma((n,)),
        ],
        compiler_params=pltpu.CompilerParams(
            collective_id=0, has_side_effects=True, vmem_limit_bytes=48 * 1024 * 1024
        ),
    )(sub_v, sub_u, sub_block, sub_count, gain_real, gain_imag, seen, rows)
    res = res.reshape(2, SG, SLOTS, SG).transpose(2, 0, 1, 3)
    return (out.reshape(ROWS, COLS, 2, FS), res.reshape(SLOTS, 2, SG * SG))


def solution(mesh):
    in_specs = (
        P("base", "facet", None, None),
        P("base", None, None),
        P("base"),
        P("base"),
        P("base"),
        P("base"),
        P(),
        P(),
    )
    out_specs = (P("base", "facet", None, None), P("base", None, None))
    return jax.shard_map(
        per_device, mesh=mesh, in_specs=in_specs, out_specs=out_specs, check_vma=False
    )
```

```python
import functools
import math

import jax
import jax.numpy as jnp
from jax import lax
from jax.experimental import pallas as pl
from jax.experimental.pallas import tpu as pltpu
from jax.sharding import PartitionSpec as P

FS = 4096
NPIX = 32768
SG = 32
NF = 16
CMAX = 4096
QUARTER = NPIX // 4
MESH = pl.DeviceIdType.MESH

LOW = 512
HIGH = FS // LOW
COLS = 4
ROWS = 8
SLOTS = 8
LANES = SLOTS * SG
STEP = 16


def cos_turns(turns):
    away = jnp.abs(((turns + NPIX // 2) & (NPIX - 1)) - NPIX // 2)
    x = (QUARTER - away).astype(jnp.float32) * (2.0 * math.pi / NPIX)
    x2 = x * x
    tail = -1.0 / 39916800
    for term in (362880, -5040, 120, -6):
        tail = tail * x2 + 1.0 / term
    return x + x * (x2 * tail)


def iota(shape, dim):
    return lax.broadcasted_iota(jnp.int32, shape, dim)


def per_lane(values, shape):
    owner = iota(shape, len(shape) - 1) // SG
    out = jnp.full(shape, values[0])
    for s in range(1, SLOTS):
        out = jnp.where(owner == s, values[s], out)
    return out


def turned(one, two, c, s):
    return one * c + two * s, two * c - one * s


def phase_plan():
    shape = (64, LANES)
    group = iota(shape, 0) // 8
    line = iota(shape, 0) % 8
    facet = (line // 2 + 2) * FS
    shift = jnp.where(line == 0, 8, 64 << line)
    distance = jnp.where(group < 2, line, jnp.where(group < 4, line * STEP, facet))
    distance = jnp.where(group < 6, distance, shift)
    sine = (group == 1) | (group == 3) | (group == 7)
    quarter = jnp.where(group == 4, -(line % 2), jnp.where(group == 5, 1 - line % 2, 0))
    return distance, jnp.where(sine, -1, quarter) * QUARTER


def fill_tables(f, distance, quarter, low, one, two):
    table = cos_turns(jnp.concatenate([f] * 8, 0) * distance[...] + quarter[...])

    def by(i):
        return table[48 + i : 49 + i], table[56 + i : 57 + i]

    def add(pair, turn):
        return pair[0] * turn[0] - pair[1] * turn[1], pair[1] * turn[0] + pair[0] * turn[1]

    fine = (table[0:8], table[8:16])
    more = add(fine, by(0))
    fine = tuple(jnp.concatenate([x, y], 0) for x, y in zip(fine, more))
    steps = [(table[16:24], table[24:32])]
    steps.append(add(steps[0], by(1)))
    steps += [add(step, by(2)) for step in steps[:2]]
    lines = [(table[32:40], table[40:48])]
    for i in range(3):
        lines += [turned(*line, *by(3 + i)) for line in lines]
    for h in range(HIGH):
        one[h] = lines[h][0]
        two[h] = lines[h][1]
    for i in range(LOW // STEP):
        step = tuple(x[i % 8 : i % 8 + 1] for x in steps[i // 8])
        cos, sin = add(fine, step)
        rows = pl.ds(i * STEP, STEP)
        low[rows, 0:LANES] = cos.astype(jnp.bfloat16)
        low[rows, LANES : 2 * LANES] = sin.astype(jnp.bfloat16)


def kernel(
    n, nf, scale,
    v_ref, u_ref, block_ref, count_ref, gain_re_ref, gain_im_ref, seen_ref, facet_ref,
    out_ref, res_ref,
    freq, distance, quarter, low_even, low_odd, one_even, one_odd, two_even, two_odd, row_table,
    seen_cells, product_even, product_odd, strip_out, strip, lift, lifted, spread_even, spread_odd,
    v_send, v_recv, s_send, s_recv, l_send, l_recv,
):
    me = lax.axis_index("base")
    mf = lax.axis_index("facet")
    pairs = n // 2

    def device(k, j):
        return {"base": lax.rem(me + k, n), "facet": lax.rem(mf + j, nf)}

    barrier = pltpu.get_barrier_semaphore()

    def greet(k, _):
        for j in range(nf):
            pl.semaphore_signal(barrier, inc=1, device_id=device(k, j), device_id_type=MESH)
        return 0

    lax.fori_loop(1, n, greet, 0)
    for j in range(1, nf):
        pl.semaphore_signal(barrier, inc=1, device_id=device(0, j), device_id_type=MESH)

    freq[me] = per_lane([v_ref[s] for s in range(SLOTS)], (8, LANES)) + iota((8, LANES), 1) % SG
    distance[...], quarter[...] = phase_plan()

    def even(i):
        return low_even.at[i], one_even.at[i], two_even.at[i]

    def odd(i):
        return low_odd.at[i], one_odd.at[i], two_odd.at[i]

    fill_tables(freq[me], distance, quarter, *even(0))

    wide = n * 2 * ROWS
    lane = iota((2 * SG, wide), 1)
    sub = iota((2 * SG, wide), 0)
    turn = (sub // SG - lane // ROWS % 2) * QUARTER
    first = (FS - n * ROWS) // 2 + lane // (2 * ROWS) * ROWS + lane % ROWS

    def fill_rows(s, _):
        u = sub % SG + u_ref[s]
        for a in range(nf):
            row_table[a, pl.ds(pl.multiple_of(s * 2 * SG, 2 * SG), 2 * SG), :] = cos_turns(
                u * (first + (a + 2) * FS) + turn
            ).astype(jnp.bfloat16)
        return 0

    lax.fori_loop(0, SLOTS, fill_rows, 0)

    owner = iota((2 * SG, LANES), 1) // SG
    cells = SG * SG
    same = iota((SG, cells), 1) // SG == iota((SG, cells), 0)
    seen = seen_ref[...].astype(jnp.float32)
    tall = jnp.concatenate(
        [jnp.where(same, seen[i : i + 1], 0.0).astype(jnp.bfloat16) for i in range(2 * SLOTS)], 0
    )
    pick = (iota((cells, LANES), 0) % SG == iota((cells, LANES), 1) % SG).astype(jnp.float32)
    picked = jnp.dot(tall, pick.astype(jnp.bfloat16), preferred_element_type=jnp.float32)
    placed = jnp.zeros((2 * SG, LANES), jnp.float32)
    for s in range(SLOTS):
        placed = jnp.where(owner == s, picked[s * 2 * SG : (s + 1) * 2 * SG], placed)
    seen_cells[...] = placed

    pl.semaphore_wait(barrier, n * nf - 1)

    def v_copy(k, slot):
        return pltpu.make_async_remote_copy(
            src_ref=freq.at[me], dst_ref=freq.at[slot], send_sem=v_send.at[k],
            recv_sem=v_recv.at[k], device_id=device(k, 0), device_id_type=MESH,
        )

    def send_v(k, _):
        v_copy(k, me).start()
        return 0

    lax.fori_loop(1, n, send_v, 0)

    def strip_copy(k, j, from_facet, from_base):
        return pltpu.make_async_remote_copy(
            src_ref=strip_out.at[k], dst_ref=strip.at[from_facet, from_base],
            send_sem=s_send.at[k, j], recv_sem=s_recv.at[k, j],
            device_id=device(k, j), device_id_type=MESH,
        )

    def multiply(low, product):
        tall = jnp.concatenate([facet_ref[:, h * LOW : (h + 1) * LOW] for h in range(HIGH)], 0)
        product[...] = jnp.dot(tall, low[...], preferred_element_type=jnp.float32)

    def fold(k, product, one, two):
        lines_re = []
        lines_im = []
        for r in range(ROWS):
            total_re = jnp.zeros((8, LANES), jnp.float32)
            total_im = jnp.zeros((8, LANES), jnp.float32)
            for h in range(HIGH):
                rows = pl.ds((h * ROWS + r) * 8, 8)
                part_cos = product[rows, 0:LANES]
                part_sin = product[rows, LANES : 2 * LANES]
                total_re = total_re + (part_cos * one[h] + part_sin * two[h])
                total_im = total_im + (part_cos * two[h] - part_sin * one[h])
            lines_re.append(jnp.sum(total_re, 0, keepdims=True))
            lines_im.append(jnp.sum(total_im, 0, keepdims=True))
        strip_out[k] = jnp.concatenate(lines_re + lines_im, 0).astype(jnp.bfloat16)

    def send_strip(k):
        @pl.when(k == 0)
        def _():
            strip[mf, me] = strip_out[k]

        @pl.when(k > 0)
        def _():
            strip_copy(k, 0, mf, me).start()

        for j in range(1, nf):
            strip_copy(k, j, mf, me).start()

    def take_v(k):
        v_copy(n - k, lax.rem(me + k, n)).wait_recv()

    def degrid(i, _):
        k = 2 * i
        take_v(k + 1)
        pl.when(k + 2 < n)(lambda: take_v(k + 2))
        low, one, two = even(i)
        multiply(low, product_even)
        fill_tables(freq[lax.rem(me + k + 1, n)], distance, quarter, *odd(i))
        fold(k, product_even, one, two)
        low, one, two = odd(i)
        multiply(low, product_odd)
        send_strip(k)
        fill_tables(freq[lax.rem(me + k + 2, n)], distance, quarter, *even(i + 1))
        fold(k + 1, product_odd, one, two)
        send_strip(k + 1)
        return 0

    lax.fori_loop(0, pairs, degrid, 0)

    half = (SG, LANES)
    gain_re = per_lane([gain_re_ref[block_ref[s]] for s in range(SLOTS)], half)
    gain_im = per_lane([gain_im_ref[block_ref[s]] for s in range(SLOTS)], half)
    weight = per_lane([count_ref[s] for s in range(SLOTS)], half).astype(jnp.float32) / CMAX
    seen = seen_cells[...]

    def take_strip(k, j):
        strip_copy(k, j, lax.rem(mf + nf - j, nf), lax.rem(me + n - k, n)).wait_recv()

    def take_strips(k, _):
        for j in range(nf):
            take_strip(k, j)
        return 0

    for j in range(1, nf):
        take_strip(0, j)
    lax.fori_loop(1, n, take_strips, 0)

    crossed = jnp.zeros((SLOTS * 2 * SG, LANES), jnp.float32)
    for a in range(nf):
        crossed = crossed + jnp.dot(
            row_table[a], strip[a].reshape(wide, LANES), preferred_element_type=jnp.float32
        )
    whole = jnp.zeros((2 * SG, LANES), jnp.float32)
    for s in range(SLOTS):
        whole = jnp.where(owner == s, crossed[s * 2 * SG : (s + 1) * 2 * SG], whole)
    whole = whole * scale
    model_re = whole[:SG]
    model_im = whole[SG:]
    diff_re = seen[:SG] - (gain_re * model_re - gain_im * model_im)
    diff_im = seen[SG:] - (gain_re * model_im + gain_im * model_re)
    res_re = weight * (gain_re * diff_re + gain_im * diff_im)
    res_im = weight * (gain_re * diff_im - gain_im * diff_re)
    residual = jnp.concatenate([res_re, res_im], 0)

    blocks = jnp.concatenate(
        [jnp.where(owner == s, residual, 0.0).astype(jnp.bfloat16) for s in range(SLOTS)], 0
    )
    raised = lax.dot_general(
        row_table[mf], blocks, (((0,), (0,)), ((), ())), preferred_element_type=jnp.float32
    )
    lift[...] = raised.astype(jnp.bfloat16).reshape(n, 2 * ROWS, LANES)

    def lift_copy(k, slot):
        return pltpu.make_async_remote_copy(
            src_ref=lift.at[lax.rem(me + k, n)], dst_ref=lifted.at[slot], send_sem=l_send.at[k],
            recv_sem=l_recv.at[k], device_id=device(k, 0), device_id_type=MESH,
        )

    def send_lift(k, _):
        lift_copy(k, me).start()
        return 0

    lax.fori_loop(1, n, send_lift, 0)
    lifted[me] = lift[me]

    grow = (iota((LANES, cells), 0) % SG == iota((LANES, cells), 1) % SG).astype(jnp.float32)
    grown = jnp.dot(blocks, grow.astype(jnp.bfloat16), preferred_element_type=jnp.float32)
    lines = [
        jnp.sum(jnp.where(same, grown[i * SG : (i + 1) * SG], 0.0), 0, keepdims=True)
        for i in range(2 * SLOTS)
    ]
    res_ref[...] = jnp.concatenate(lines, 0).astype(jnp.bfloat16)

    def turn_chunk(k, one, two, spread):
        value = lifted[lax.rem(me + n - k, n)].astype(jnp.float32) * scale
        for h in range(HIGH):
            for r in range(0, ROWS, 2):
                by_cos = []
                by_sin = []
                for t in (r, r + 1):
                    re = value[t : t + 1]
                    im = value[ROWS + t : ROWS + t + 1]
                    by_cos.append(re * one[h] + im * two[h])
                    by_sin.append(re * two[h] - im * one[h])
                rows = pl.ds((h * ROWS + r) * 8, 16)
                spread[rows, 0:LANES] = jnp.concatenate(by_cos, 0).astype(jnp.bfloat16)
                spread[rows, LANES : 2 * LANES] = jnp.concatenate(by_sin, 0).astype(jnp.bfloat16)

    def gather(spread, low):
        term = lax.dot_general(
            spread[...], low[...], (((1,), (1,)), ((), ())), preferred_element_type=jnp.float32
        )
        for h in range(HIGH):
            out_ref[:, pl.ds(h * LOW, LOW)] += term[h * 8 * ROWS : (h + 1) * 8 * ROWS]

    def take_lift(k):
        lift_copy(k, lax.rem(me + n - k, n)).wait_recv()

    def grid(i, _):
        k = 2 * i
        take_lift(k + 1)
        low, one, two = odd(pairs - i - 1)
        gather(spread_even, low_even.at[pairs - i])
        turn_chunk(k + 1, one, two, spread_odd)
        pl.when(k + 2 < n)(lambda: take_lift(k + 2))
        gather(spread_odd, low)
        _, one, two = even(pairs - i - 1)
        turn_chunk(lax.rem(k + 2, n), one, two, spread_even)
        return 0

    out_ref[...] = jnp.zeros(out_ref.shape, jnp.float32)
    _, one, two = even(pairs)
    turn_chunk(0, one, two, spread_even)
    lax.fori_loop(0, pairs, grid, 0)

    def drain(k, _):
        v_copy(k, me).wait_send()
        lift_copy(k, me).wait_send()
        for j in range(nf):
            strip_copy(k, j, mf, me).wait_send()
        return 0

    lax.fori_loop(1, n, drain, 0)
    for j in range(1, nf):
        strip_copy(0, j, mf, me).wait_send()


def per_device(facets, observed, sub_u, sub_v, sub_block, sub_count, gain_real, gain_imag):
    n = lax.axis_size("base")
    nf = lax.axis_size("facet")
    assert facets.shape == (ROWS, COLS, 2, FS) and nf * COLS == NF and n % 2 == 0
    assert observed.shape == (SLOTS, 2, SG * SG)
    scale = 1.0 / math.sqrt(NF * n * ROWS * FS)
    rows = facets.reshape(ROWS * COLS * 2, FS)
    seen = observed.reshape(SLOTS * 2, SG * SG)
    smem = pl.BlockSpec(memory_space=pltpu.SMEM)
    vmem = pl.BlockSpec(memory_space=pltpu.VMEM)
    bf16 = jnp.bfloat16
    f32 = jnp.float32
    dma = pltpu.SemaphoreType.DMA
    out, res = pl.pallas_call(
        functools.partial(kernel, n, nf, scale),
        out_shape=(
            jax.ShapeDtypeStruct((ROWS * COLS * 2, FS), f32),
            jax.ShapeDtypeStruct((SLOTS * 2, SG * SG), bf16),
        ),
        in_specs=[smem] * 6 + [vmem] * 2,
        out_specs=(vmem, vmem),
        scratch_shapes=[
            pltpu.VMEM((n, 8, LANES), jnp.int32),
            pltpu.VMEM((64, LANES), jnp.int32),
            pltpu.VMEM((64, LANES), jnp.int32),
            pltpu.VMEM((n // 2 + 1, LOW, 2 * LANES), bf16),
            pltpu.VMEM((n // 2, LOW, 2 * LANES), bf16),
            pltpu.VMEM((n // 2 + 1, HIGH, 8, LANES), f32),
            pltpu.VMEM((n // 2, HIGH, 8, LANES), f32),
            pltpu.VMEM((n // 2 + 1, HIGH, 8, LANES), f32),
            pltpu.VMEM((n // 2, HIGH, 8, LANES), f32),
            pltpu.VMEM((nf, SLOTS * 2 * SG, n * 2 * ROWS), bf16),
            pltpu.VMEM((2 * SG, LANES), f32),
            pltpu.VMEM((HIGH * ROWS * 8, 2 * LANES), f32),
            pltpu.VMEM((HIGH * ROWS * 8, 2 * LANES), f32),
            pltpu.VMEM((n, 2 * ROWS, LANES), bf16),
            pltpu.VMEM((nf, n, 2 * ROWS, LANES), bf16),
            pltpu.VMEM((n, 2 * ROWS, LANES), bf16),
            pltpu.VMEM((n, 2 * ROWS, LANES), bf16),
            pltpu.VMEM((HIGH * ROWS * 8, 2 * LANES), bf16),
            pltpu.VMEM((HIGH * ROWS * 8, 2 * LANES), bf16),
            dma((n,)), dma((n,)), dma((n, nf)), dma((n, nf)), dma((n,)), dma((n,)),
        ],
        compiler_params=pltpu.CompilerParams(
            collective_id=0, has_side_effects=True, vmem_limit_bytes=48 * 1024 * 1024
        ),
    )(sub_v, sub_u, sub_block, sub_count, gain_real, gain_imag, seen, rows)
    return (out.reshape(ROWS, COLS, 2, FS), res.reshape(SLOTS, 2, SG * SG))


def solution(mesh):
    in_specs = (
        P("base", "facet", None, None),
        P("base", None, None),
        P("base"),
        P("base"),
        P("base"),
        P("base"),
        P(),
        P(),
    )
    out_specs = (P("base", "facet", None, None), P("base", None, None))
    return jax.shard_map(
        per_device, mesh=mesh, in_specs=in_specs, out_specs=out_specs, check_vma=False
    )
```

```python
import functools
import math

import jax
import jax.numpy as jnp
from jax import lax
from jax.experimental import pallas as pl
from jax.experimental.pallas import tpu as pltpu
from jax.sharding import PartitionSpec as P

FS = 4096
NPIX = 32768
SG = 32
NF = 16
CMAX = 4096
QUARTER = NPIX // 4
MESH = pl.DeviceIdType.MESH

LOW = 512
HIGH = FS // LOW
COLS = 4
ROWS = 8
SLOTS = 8
LANES = SLOTS * SG
STEP = 16


def cos_turns(turns):
    away = jnp.abs(((turns + NPIX // 2) & (NPIX - 1)) - NPIX // 2)
    x = (QUARTER - away).astype(jnp.float32) * (2.0 * math.pi / NPIX)
    x2 = x * x
    tail = -1.0 / 39916800
    for term in (362880, -5040, 120, -6):
        tail = tail * x2 + 1.0 / term
    return x + x * (x2 * tail)


def iota(shape, dim):
    return lax.broadcasted_iota(jnp.int32, shape, dim)


def per_lane(values, shape):
    owner = iota(shape, len(shape) - 1) // SG
    out = jnp.full(shape, values[0])
    for s in range(1, SLOTS):
        out = jnp.where(owner == s, values[s], out)
    return out


def turned(one, two, c, s):
    return one * c + two * s, two * c - one * s


def phase_plan():
    shape = (64, LANES)
    group = iota(shape, 0) // 8
    line = iota(shape, 0) % 8
    facet = (line // 2 + 2) * FS
    shift = jnp.where(line == 0, 8, 64 << line)
    distance = jnp.where(group < 2, line, jnp.where(group < 4, line * STEP, facet))
    distance = jnp.where(group < 6, distance, shift)
    sine = (group == 1) | (group == 3) | (group == 7)
    quarter = jnp.where(group == 4, -(line % 2), jnp.where(group == 5, 1 - line % 2, 0))
    return distance, jnp.where(sine, -1, quarter) * QUARTER


def fill_tables(f, distance, quarter, low, one, two):
    table = cos_turns(jnp.concatenate([f] * 8, 0) * distance[...] + quarter[...])

    def by(i):
        return table[48 + i : 49 + i], table[56 + i : 57 + i]

    def add(pair, turn):
        return pair[0] * turn[0] - pair[1] * turn[1], pair[1] * turn[0] + pair[0] * turn[1]

    fine = (table[0:8], table[8:16])
    more = add(fine, by(0))
    fine = tuple(jnp.concatenate([x, y], 0) for x, y in zip(fine, more))
    steps = [(table[16:24], table[24:32])]
    steps.append(add(steps[0], by(1)))
    steps += [add(step, by(2)) for step in steps[:2]]
    lines = [(table[32:40], table[40:48])]
    for i in range(3):
        lines += [turned(*line, *by(3 + i)) for line in lines]
    for h in range(HIGH):
        one[h] = lines[h][0]
        two[h] = lines[h][1]
    for i in range(LOW // STEP):
        step = tuple(x[i % 8 : i % 8 + 1] for x in steps[i // 8])
        cos, sin = add(fine, step)
        rows = pl.ds(i * STEP, STEP)
        low[rows, 0:LANES] = cos.astype(jnp.bfloat16)
        low[rows, LANES : 2 * LANES] = sin.astype(jnp.bfloat16)


def kernel(
    n, nf, scale,
    v_raw, u_raw, block_raw, count_raw, gain_re_raw, gain_im_raw, seen_raw, facet_raw,
    out_ref, res_ref,
    v_ref, u_ref, block_ref, count_ref, gain_re_ref, gain_im_ref, seen_ref, facet_four,
    facet_ref, freq, distance, quarter, low_even, low_odd, one_even, one_odd, two_even, two_odd, row_table,
    seen_cells, product_even, product_odd, strip_out, strip, lift, lifted, spread_even, spread_odd,
    v_send, v_recv, s_send, s_recv, l_send, l_recv, in_sem,
):
    me = lax.axis_index("base")
    mf = lax.axis_index("facet")
    pairs = n // 2

    def device(k, j):
        return {"base": lax.rem(me + k, n), "facet": lax.rem(mf + j, nf)}

    raw = [v_raw, facet_raw, seen_raw, u_raw, block_raw, count_raw, gain_re_raw, gain_im_raw]
    held = [v_ref, facet_four, seen_ref, u_ref, block_ref, count_ref, gain_re_ref, gain_im_ref]
    loads = [
        pltpu.make_async_copy(src, dst, in_sem.at[i]) for i, (src, dst) in enumerate(zip(raw, held))
    ]
    for load in loads:
        load.start()

    barrier = pltpu.get_barrier_semaphore()

    def greet(k, _):
        for j in range(nf):
            pl.semaphore_signal(barrier, inc=1, device_id=device(k, j), device_id_type=MESH)
        return 0

    lax.fori_loop(1, n, greet, 0)
    for j in range(1, nf):
        pl.semaphore_signal(barrier, inc=1, device_id=device(0, j), device_id_type=MESH)

    loads[0].wait()
    freq[me] = per_lane([v_ref[s] for s in range(SLOTS)], (8, LANES)) + iota((8, LANES), 1) % SG
    distance[...], quarter[...] = phase_plan()

    def even(i):
        return low_even.at[i], one_even.at[i], two_even.at[i]

    def odd(i):
        return low_odd.at[i], one_odd.at[i], two_odd.at[i]


    loads[1].wait()
    for r in range(0, ROWS, 2):
        both = []
        for t in (r, r + 1):
            both += [facet_four[t, b].astype(jnp.float32) for b in range(COLS)]
        facet_ref[pl.ds(r * 8, 16), :] = jnp.concatenate(both, 0).astype(jnp.bfloat16)

    pl.semaphore_wait(barrier, n * nf - 1)

    def v_copy(k, slot):
        return pltpu.make_async_remote_copy(
            src_ref=freq.at[me], dst_ref=freq.at[slot], send_sem=v_send.at[k],
            recv_sem=v_recv.at[k], device_id=device(k, 0), device_id_type=MESH,
        )

    def send_v(k, _):
        v_copy(k, me).start()
        return 0

    lax.fori_loop(1, n, send_v, 0)

    fill_tables(freq[me], distance, quarter, *even(0))

    for load in loads[2:]:
        load.wait()

    wide = n * 2 * ROWS
    lane = iota((2 * SG, wide), 1)
    sub = iota((2 * SG, wide), 0)
    turn = (sub // SG - lane // ROWS % 2) * QUARTER
    first = (FS - n * ROWS) // 2 + lane // (2 * ROWS) * ROWS + lane % ROWS

    def fill_rows(s, _):
        u = sub % SG + u_ref[s]
        for a in range(nf):
            row_table[a, pl.ds(pl.multiple_of(s * 2 * SG, 2 * SG), 2 * SG), :] = cos_turns(
                u * (first + (a + 2) * FS) + turn
            ).astype(jnp.bfloat16)
        return 0

    lax.fori_loop(0, SLOTS, fill_rows, 0)

    owner = iota((2 * SG, LANES), 1) // SG
    cells = SG * SG
    same = iota((SG, cells), 1) // SG == iota((SG, cells), 0)
    tall = []
    for s in range(SLOTS):
        seen = seen_ref[s].astype(jnp.float32)
        tall += [jnp.where(same, seen[i : i + 1], 0.0).astype(jnp.bfloat16) for i in range(2)]
    tall = jnp.concatenate(tall, 0)
    pick = (iota((cells, LANES), 0) % SG == iota((cells, LANES), 1) % SG).astype(jnp.float32)
    picked = jnp.dot(tall, pick.astype(jnp.bfloat16), preferred_element_type=jnp.float32)
    placed = jnp.zeros((2 * SG, LANES), jnp.float32)
    for s in range(SLOTS):
        placed = jnp.where(owner == s, picked[s * 2 * SG : (s + 1) * 2 * SG], placed)
    seen_cells[...] = placed

    def strip_copy(k, j, from_facet, from_base):
        return pltpu.make_async_remote_copy(
            src_ref=strip_out.at[k], dst_ref=strip.at[from_facet, from_base],
            send_sem=s_send.at[k, j], recv_sem=s_recv.at[k, j],
            device_id=device(k, j), device_id_type=MESH,
        )

    def multiply(low, product):
        tall = jnp.concatenate([facet_ref[:, h * LOW : (h + 1) * LOW] for h in range(HIGH)], 0)
        product[...] = jnp.dot(tall, low[...], preferred_element_type=jnp.float32)

    def fold(k, product, one, two):
        lines_re = []
        lines_im = []
        for r in range(ROWS):
            total_re = jnp.zeros((8, LANES), jnp.float32)
            total_im = jnp.zeros((8, LANES), jnp.float32)
            for h in range(HIGH):
                rows = pl.ds((h * ROWS + r) * 8, 8)
                part_cos = product[rows, 0:LANES]
                part_sin = product[rows, LANES : 2 * LANES]
                total_re = total_re + (part_cos * one[h] + part_sin * two[h])
                total_im = total_im + (part_cos * two[h] - part_sin * one[h])
            lines_re.append(jnp.sum(total_re, 0, keepdims=True))
            lines_im.append(jnp.sum(total_im, 0, keepdims=True))
        strip_out[k] = jnp.concatenate(lines_re + lines_im, 0).astype(jnp.bfloat16)

    def send_strip(k):
        @pl.when(k == 0)
        def _():
            strip[mf, me] = strip_out[k]

        @pl.when(k > 0)
        def _():
            strip_copy(k, 0, mf, me).start()

        for j in range(1, nf):
            strip_copy(k, j, mf, me).start()

    def take_v(k):
        v_copy(n - k, lax.rem(me + k, n)).wait_recv()

    def degrid(i, _):
        k = 2 * i
        low, one, two = even(i)
        multiply(low, product_even)
        take_v(k + 1)
        pl.when(k + 2 < n)(lambda: take_v(k + 2))
        fill_tables(freq[lax.rem(me + k + 1, n)], distance, quarter, *odd(i))
        fold(k, product_even, one, two)
        low, one, two = odd(i)
        multiply(low, product_odd)
        send_strip(k)
        fill_tables(freq[lax.rem(me + k + 2, n)], distance, quarter, *even(i + 1))
        fold(k + 1, product_odd, one, two)
        send_strip(k + 1)
        return 0

    lax.fori_loop(0, pairs, degrid, 0)

    half = (SG, LANES)
    gain_re = per_lane([gain_re_ref[block_ref[s]] for s in range(SLOTS)], half)
    gain_im = per_lane([gain_im_ref[block_ref[s]] for s in range(SLOTS)], half)
    weight = per_lane([count_ref[s] for s in range(SLOTS)], half).astype(jnp.float32) / CMAX
    seen = seen_cells[...]

    def take_strip(k, j):
        strip_copy(k, j, lax.rem(mf + nf - j, nf), lax.rem(me + n - k, n)).wait_recv()

    def take_strips(k, _):
        for j in range(nf):
            take_strip(k, j)
        return 0

    for j in range(1, nf):
        take_strip(0, j)
    lax.fori_loop(1, n, take_strips, 0)

    crossed = jnp.zeros((SLOTS * 2 * SG, LANES), jnp.float32)
    for a in range(nf):
        crossed = crossed + jnp.dot(
            row_table[a], strip[a].reshape(wide, LANES), preferred_element_type=jnp.float32
        )
    whole = jnp.zeros((2 * SG, LANES), jnp.float32)
    for s in range(SLOTS):
        whole = jnp.where(owner == s, crossed[s * 2 * SG : (s + 1) * 2 * SG], whole)
    whole = whole * scale
    model_re = whole[:SG]
    model_im = whole[SG:]
    diff_re = seen[:SG] - (gain_re * model_re - gain_im * model_im)
    diff_im = seen[SG:] - (gain_re * model_im + gain_im * model_re)
    res_re = weight * (gain_re * diff_re + gain_im * diff_im)
    res_im = weight * (gain_re * diff_im - gain_im * diff_re)
    residual = jnp.concatenate([res_re, res_im], 0)

    blocks = jnp.concatenate(
        [jnp.where(owner == s, residual, 0.0).astype(jnp.bfloat16) for s in range(SLOTS)], 0
    )
    raised = lax.dot_general(
        row_table[mf], blocks, (((0,), (0,)), ((), ())), preferred_element_type=jnp.float32
    )
    lift[...] = raised.astype(jnp.bfloat16).reshape(n, 2 * ROWS, LANES)

    def lift_copy(k, slot):
        return pltpu.make_async_remote_copy(
            src_ref=lift.at[lax.rem(me + k, n)], dst_ref=lifted.at[slot], send_sem=l_send.at[k],
            recv_sem=l_recv.at[k], device_id=device(k, 0), device_id_type=MESH,
        )

    def send_lift(k, _):
        lift_copy(k, me).start()
        return 0

    lax.fori_loop(1, n, send_lift, 0)
    lifted[me] = lift[me]

    grow = (iota((LANES, cells), 0) % SG == iota((LANES, cells), 1) % SG).astype(jnp.float32)
    grown = jnp.dot(blocks, grow.astype(jnp.bfloat16), preferred_element_type=jnp.float32)
    lines = [
        jnp.sum(jnp.where(same, grown[i * SG : (i + 1) * SG], 0.0), 0, keepdims=True)
        for i in range(2 * SLOTS)
    ]
    res_ref[...] = jnp.concatenate(lines, 0).astype(jnp.bfloat16)

    def turn_chunk(k, one, two, spread):
        value = lifted[lax.rem(me + n - k, n)].astype(jnp.float32) * scale
        for h in range(HIGH):
            for r in range(0, ROWS, 2):
                by_cos = []
                by_sin = []
                for t in (r, r + 1):
                    re = value[t : t + 1]
                    im = value[ROWS + t : ROWS + t + 1]
                    by_cos.append(re * one[h] + im * two[h])
                    by_sin.append(re * two[h] - im * one[h])
                rows = pl.ds((h * ROWS + r) * 8, 16)
                spread[rows, 0:LANES] = jnp.concatenate(by_cos, 0).astype(jnp.bfloat16)
                spread[rows, LANES : 2 * LANES] = jnp.concatenate(by_sin, 0).astype(jnp.bfloat16)

    def gather(spread, low):
        term = lax.dot_general(
            spread[...], low[...], (((1,), (1,)), ((), ())), preferred_element_type=jnp.float32
        )
        for h in range(HIGH):
            out_ref[:, pl.ds(h * LOW, LOW)] += term[h * 8 * ROWS : (h + 1) * 8 * ROWS]

    def take_lift(k):
        lift_copy(k, lax.rem(me + n - k, n)).wait_recv()

    def grid(i, _):
        k = 2 * i
        take_lift(k + 1)
        low, one, two = odd(pairs - i - 1)
        gather(spread_even, low_even.at[pairs - i])
        turn_chunk(k + 1, one, two, spread_odd)
        pl.when(k + 2 < n)(lambda: take_lift(k + 2))
        gather(spread_odd, low)
        _, one, two = even(pairs - i - 1)
        turn_chunk(lax.rem(k + 2, n), one, two, spread_even)
        return 0

    out_ref[...] = jnp.zeros(out_ref.shape, jnp.float32)
    _, one, two = even(pairs)
    turn_chunk(0, one, two, spread_even)
    lax.fori_loop(0, pairs, grid, 0)

    def drain(k, _):
        v_copy(k, me).wait_send()
        lift_copy(k, me).wait_send()
        for j in range(nf):
            strip_copy(k, j, mf, me).wait_send()
        return 0

    lax.fori_loop(1, n, drain, 0)
    for j in range(1, nf):
        strip_copy(0, j, mf, me).wait_send()


def per_device(facets, observed, sub_u, sub_v, sub_block, sub_count, gain_real, gain_imag):
    n = lax.axis_size("base")
    nf = lax.axis_size("facet")
    assert facets.shape == (ROWS, COLS, 2, FS) and nf * COLS == NF and n % 2 == 0
    assert observed.shape == (SLOTS, 2, SG * SG)
    scale = 1.0 / math.sqrt(NF * n * ROWS * FS)
    hbm = pl.BlockSpec(memory_space=pltpu.HBM)
    vmem = pl.BlockSpec(memory_space=pltpu.VMEM)
    bf16 = jnp.bfloat16
    f32 = jnp.float32
    dma = pltpu.SemaphoreType.DMA
    out, res = pl.pallas_call(
        functools.partial(kernel, n, nf, scale),
        out_shape=(
            jax.ShapeDtypeStruct((ROWS * COLS * 2, FS), f32),
            jax.ShapeDtypeStruct((SLOTS * 2, SG * SG), bf16),
        ),
        in_specs=[hbm] * 8,
        out_specs=(vmem, vmem),
        scratch_shapes=[
            pltpu.SMEM((SLOTS,), jnp.int32),
            pltpu.SMEM((SLOTS,), jnp.int32),
            pltpu.SMEM((SLOTS,), jnp.int32),
            pltpu.SMEM((SLOTS,), jnp.int32),
            pltpu.SMEM(gain_real.shape, f32),
            pltpu.SMEM(gain_imag.shape, f32),
            pltpu.VMEM(observed.shape, bf16),
            pltpu.VMEM(facets.shape, bf16),
            pltpu.VMEM((ROWS * COLS * 2, FS), bf16),
            pltpu.VMEM((n, 8, LANES), jnp.int32),
            pltpu.VMEM((64, LANES), jnp.int32),
            pltpu.VMEM((64, LANES), jnp.int32),
            pltpu.VMEM((n // 2 + 1, LOW, 2 * LANES), bf16),
            pltpu.VMEM((n // 2, LOW, 2 * LANES), bf16),
            pltpu.VMEM((n // 2 + 1, HIGH, 8, LANES), f32),
            pltpu.VMEM((n // 2, HIGH, 8, LANES), f32),
            pltpu.VMEM((n // 2 + 1, HIGH, 8, LANES), f32),
            pltpu.VMEM((n // 2, HIGH, 8, LANES), f32),
            pltpu.VMEM((nf, SLOTS * 2 * SG, n * 2 * ROWS), bf16),
            pltpu.VMEM((2 * SG, LANES), f32),
            pltpu.VMEM((HIGH * ROWS * 8, 2 * LANES), f32),
            pltpu.VMEM((HIGH * ROWS * 8, 2 * LANES), f32),
            pltpu.VMEM((n, 2 * ROWS, LANES), bf16),
            pltpu.VMEM((nf, n, 2 * ROWS, LANES), bf16),
            pltpu.VMEM((n, 2 * ROWS, LANES), bf16),
            pltpu.VMEM((n, 2 * ROWS, LANES), bf16),
            pltpu.VMEM((HIGH * ROWS * 8, 2 * LANES), bf16),
            pltpu.VMEM((HIGH * ROWS * 8, 2 * LANES), bf16),
            dma((n,)), dma((n,)), dma((n, nf)), dma((n, nf)), dma((n,)), dma((n,)), dma((8,)),
        ],
        compiler_params=pltpu.CompilerParams(
            collective_id=0, has_side_effects=True, vmem_limit_bytes=48 * 1024 * 1024
        ),
    )(sub_v, sub_u, sub_block, sub_count, gain_real, gain_imag, observed, facets)
    return (out.reshape(ROWS, COLS, 2, FS), res.reshape(SLOTS, 2, SG * SG))


def solution(mesh):
    in_specs = (
        P("base", "facet", None, None),
        P("base", None, None),
        P("base"),
        P("base"),
        P("base"),
        P("base"),
        P(),
        P(),
    )
    out_specs = (P("base", "facet", None, None), P("base", None, None))
    return jax.shard_map(
        per_device, mesh=mesh, in_specs=in_specs, out_specs=out_specs, check_vma=False
    )
```

```python
import functools
import math

import jax
import jax.numpy as jnp
from jax import lax
from jax.experimental import pallas as pl
from jax.experimental.pallas import tpu as pltpu
from jax.sharding import PartitionSpec as P

FS = 4096
NPIX = 32768
SG = 32
NF = 16
CMAX = 4096
QUARTER = NPIX // 4
MESH = pl.DeviceIdType.MESH

LOW = 512
HIGH = FS // LOW
COLS = 4
ROWS = 8
SLOTS = 8
LANES = SLOTS * SG
STEP = 16


def cos_turns(turns):
    away = jnp.abs(((turns + NPIX // 2) & (NPIX - 1)) - NPIX // 2)
    x = (QUARTER - away).astype(jnp.float32) * (2.0 * math.pi / NPIX)
    x2 = x * x
    tail = -1.0 / 39916800
    for term in (362880, -5040, 120, -6):
        tail = tail * x2 + 1.0 / term
    return x + x * (x2 * tail)


def iota(shape, dim):
    return lax.broadcasted_iota(jnp.int32, shape, dim)


def per_lane(values, shape):
    owner = iota(shape, len(shape) - 1) // SG
    out = jnp.full(shape, values[0])
    for s in range(1, SLOTS):
        out = jnp.where(owner == s, values[s], out)
    return out


def turned(one, two, c, s):
    return one * c + two * s, two * c - one * s


def phase_plan():
    shape = (64, LANES)
    group = iota(shape, 0) // 8
    line = iota(shape, 0) % 8
    facet = (line // 2 + 2) * FS
    shift = jnp.where(line == 0, 8, 64 << line)
    distance = jnp.where(group < 2, line, jnp.where(group < 4, line * STEP, facet))
    distance = jnp.where(group < 6, distance, shift)
    sine = (group == 1) | (group == 3) | (group == 7)
    quarter = jnp.where(group == 4, -(line % 2), jnp.where(group == 5, 1 - line % 2, 0))
    return distance, jnp.where(sine, -1, quarter) * QUARTER


def fill_tables(f, distance, quarter, low, one, two):
    table = cos_turns(jnp.concatenate([f] * 8, 0) * distance[...] + quarter[...])

    def by(i):
        return table[48 + i : 49 + i], table[56 + i : 57 + i]

    def add(pair, turn):
        return pair[0] * turn[0] - pair[1] * turn[1], pair[1] * turn[0] + pair[0] * turn[1]

    fine = (table[0:8], table[8:16])
    more = add(fine, by(0))
    fine = tuple(jnp.concatenate([x, y], 0) for x, y in zip(fine, more))
    steps = [(table[16:24], table[24:32])]
    steps.append(add(steps[0], by(1)))
    steps += [add(step, by(2)) for step in steps[:2]]
    lines = [(table[32:40], table[40:48])]
    for i in range(3):
        lines += [turned(*line, *by(3 + i)) for line in lines]
    for h in range(HIGH):
        one[h] = lines[h][0]
        two[h] = lines[h][1]
    for i in range(LOW // STEP):
        step = tuple(x[i % 8 : i % 8 + 1] for x in steps[i // 8])
        cos, sin = add(fine, step)
        rows = pl.ds(i * STEP, STEP)
        low[rows, 0:LANES] = cos.astype(jnp.bfloat16)
        low[rows, LANES : 2 * LANES] = sin.astype(jnp.bfloat16)


def kernel(
    n, nf, scale,
    v_raw, u_raw, block_raw, count_raw, gain_re_raw, gain_im_raw, seen_raw, facet_raw,
    out_ref, res_ref,
    v_ref, u_ref, block_ref, count_ref, gain_re_ref, gain_im_ref, seen_ref, facet_four,
    facet_ref, freq, distance, quarter, low_even, low_odd, one_even, one_odd, two_even, two_odd, row_table,
    seen_cells, product_even, product_odd, strip_out, strip, model, lift, lifted, spread_even, spread_odd,
    v_send, v_recv, s_send, s_recv, m_send, m_recv, l_send, l_recv, in_sem,
):
    me = lax.axis_index("base")
    mf = lax.axis_index("facet")
    pairs = n // 2

    def device(k, j):
        return {"base": lax.rem(me + k, n), "facet": lax.rem(mf + j, nf)}

    raw = [v_raw, facet_raw, seen_raw, u_raw, block_raw, count_raw, gain_re_raw, gain_im_raw]
    held = [v_ref, facet_four, seen_ref, u_ref, block_ref, count_ref, gain_re_ref, gain_im_ref]
    loads = [
        pltpu.make_async_copy(src, dst, in_sem.at[i]) for i, (src, dst) in enumerate(zip(raw, held))
    ]
    for load in loads:
        load.start()

    barrier = pltpu.get_barrier_semaphore()

    def greet(k, _):
        pl.semaphore_signal(barrier, inc=1, device_id=device(k, 0), device_id_type=MESH)
        return 0

    lax.fori_loop(1, n, greet, 0)
    for j in range(1, nf):
        pl.semaphore_signal(barrier, inc=1, device_id=device(0, j), device_id_type=MESH)

    loads[0].wait()
    freq[me] = per_lane([v_ref[s] for s in range(SLOTS)], (8, LANES)) + iota((8, LANES), 1) % SG
    distance[...], quarter[...] = phase_plan()

    def even(i):
        return low_even.at[i], one_even.at[i], two_even.at[i]

    def odd(i):
        return low_odd.at[i], one_odd.at[i], two_odd.at[i]


    loads[1].wait()
    for r in range(0, ROWS, 2):
        both = []
        for t in (r, r + 1):
            both += [facet_four[t, b].astype(jnp.float32) for b in range(COLS)]
        facet_ref[pl.ds(r * 8, 16), :] = jnp.concatenate(both, 0).astype(jnp.bfloat16)

    pl.semaphore_wait(barrier, n - 1 + nf - 1)

    def v_copy(k, slot):
        return pltpu.make_async_remote_copy(
            src_ref=freq.at[me], dst_ref=freq.at[slot], send_sem=v_send.at[k],
            recv_sem=v_recv.at[k], device_id=device(k, 0), device_id_type=MESH,
        )

    def send_v(k, _):
        v_copy(k, me).start()
        return 0

    lax.fori_loop(1, n, send_v, 0)

    fill_tables(freq[me], distance, quarter, *even(0))

    for load in loads[2:]:
        load.wait()

    wide = n * 2 * ROWS
    lane = iota((2 * SG, wide), 1)
    sub = iota((2 * SG, wide), 0)
    turn = (sub // SG - lane // ROWS % 2) * QUARTER
    first = (FS - n * ROWS) // 2 + lane // (2 * ROWS) * ROWS + lane % ROWS

    place = first + (mf + 2) * FS

    def fill_rows(s, _):
        row_table[pl.ds(pl.multiple_of(s * 2 * SG, 2 * SG), 2 * SG), :] = cos_turns(
            (sub % SG + u_ref[s]) * place + turn
        ).astype(jnp.bfloat16)
        return 0

    lax.fori_loop(0, SLOTS, fill_rows, 0)

    owner = iota((2 * SG, LANES), 1) // SG
    cells = SG * SG
    same = iota((SG, cells), 1) // SG == iota((SG, cells), 0)
    tall = []
    for s in range(SLOTS):
        seen = seen_ref[s].astype(jnp.float32)
        tall += [jnp.where(same, seen[i : i + 1], 0.0).astype(jnp.bfloat16) for i in range(2)]
    tall = jnp.concatenate(tall, 0)
    pick = (iota((cells, LANES), 0) % SG == iota((cells, LANES), 1) % SG).astype(jnp.float32)
    picked = jnp.dot(tall, pick.astype(jnp.bfloat16), preferred_element_type=jnp.float32)
    placed = jnp.zeros((2 * SG, LANES), jnp.float32)
    for s in range(SLOTS):
        placed = jnp.where(owner == s, picked[s * 2 * SG : (s + 1) * 2 * SG], placed)
    seen_cells[...] = placed

    def strip_copy(k, slot):
        return pltpu.make_async_remote_copy(
            src_ref=strip_out.at[k], dst_ref=strip.at[slot], send_sem=s_send.at[k],
            recv_sem=s_recv.at[k], device_id=device(k, 0), device_id_type=MESH,
        )

    def model_copy(j, slot):
        return pltpu.make_async_remote_copy(
            src_ref=model.at[mf], dst_ref=model.at[slot], send_sem=m_send.at[j],
            recv_sem=m_recv.at[j], device_id=device(0, j), device_id_type=MESH,
        )

    def multiply(low, product):
        tall = jnp.concatenate([facet_ref[:, h * LOW : (h + 1) * LOW] for h in range(HIGH)], 0)
        product[...] = jnp.dot(tall, low[...], preferred_element_type=jnp.float32)

    def fold(k, product, one, two):
        lines_re = []
        lines_im = []
        for r in range(ROWS):
            total_re = jnp.zeros((8, LANES), jnp.float32)
            total_im = jnp.zeros((8, LANES), jnp.float32)
            for h in range(HIGH):
                rows = pl.ds((h * ROWS + r) * 8, 8)
                part_cos = product[rows, 0:LANES]
                part_sin = product[rows, LANES : 2 * LANES]
                total_re = total_re + (part_cos * one[h] + part_sin * two[h])
                total_im = total_im + (part_cos * two[h] - part_sin * one[h])
            lines_re.append(jnp.sum(total_re, 0, keepdims=True))
            lines_im.append(jnp.sum(total_im, 0, keepdims=True))
        strip_out[k] = jnp.concatenate(lines_re + lines_im, 0).astype(jnp.bfloat16)

    def send_strip(k):
        @pl.when(k == 0)
        def _():
            strip[me] = strip_out[k]

        @pl.when(k > 0)
        def _():
            strip_copy(k, me).start()

    def take_v(k):
        v_copy(n - k, lax.rem(me + k, n)).wait_recv()

    def degrid(i, _):
        k = 2 * i
        low, one, two = even(i)
        multiply(low, product_even)
        take_v(k + 1)
        pl.when(k + 2 < n)(lambda: take_v(k + 2))
        fill_tables(freq[lax.rem(me + k + 1, n)], distance, quarter, *odd(i))
        fold(k, product_even, one, two)
        low, one, two = odd(i)
        multiply(low, product_odd)
        send_strip(k)
        fill_tables(freq[lax.rem(me + k + 2, n)], distance, quarter, *even(i + 1))
        fold(k + 1, product_odd, one, two)
        send_strip(k + 1)
        return 0

    lax.fori_loop(0, pairs, degrid, 0)

    half = (SG, LANES)
    gain_re = per_lane([gain_re_ref[block_ref[s]] for s in range(SLOTS)], half)
    gain_im = per_lane([gain_im_ref[block_ref[s]] for s in range(SLOTS)], half)
    weight = per_lane([count_ref[s] for s in range(SLOTS)], half).astype(jnp.float32) / CMAX
    seen = seen_cells[...]

    def take_strip(k, _):
        strip_copy(k, lax.rem(me + n - k, n)).wait_recv()
        return 0

    lax.fori_loop(1, n, take_strip, 0)

    crossed = jnp.dot(
        row_table[...], strip[...].reshape(wide, LANES), preferred_element_type=jnp.float32
    )
    part = jnp.zeros((2 * SG, LANES), jnp.float32)
    for s in range(SLOTS):
        part = jnp.where(owner == s, crossed[s * 2 * SG : (s + 1) * 2 * SG], part)
    model[mf] = (part * scale).astype(jnp.bfloat16)
    for j in range(1, nf):
        model_copy(j, mf).start()
    for j in range(1, nf):
        model_copy(j, lax.rem(mf + nf - j, nf)).wait_recv()
    whole = model[0].astype(jnp.float32)
    for j in range(1, nf):
        whole = whole + model[j].astype(jnp.float32)
    model_re = whole[:SG]
    model_im = whole[SG:]
    diff_re = seen[:SG] - (gain_re * model_re - gain_im * model_im)
    diff_im = seen[SG:] - (gain_re * model_im + gain_im * model_re)
    res_re = weight * (gain_re * diff_re + gain_im * diff_im)
    res_im = weight * (gain_re * diff_im - gain_im * diff_re)
    residual = jnp.concatenate([res_re, res_im], 0)

    blocks = jnp.concatenate(
        [jnp.where(owner == s, residual, 0.0).astype(jnp.bfloat16) for s in range(SLOTS)], 0
    )
    raised = lax.dot_general(
        row_table[...], blocks, (((0,), (0,)), ((), ())), preferred_element_type=jnp.float32
    )
    lift[...] = raised.astype(jnp.bfloat16).reshape(n, 2 * ROWS, LANES)

    def lift_copy(k, slot):
        return pltpu.make_async_remote_copy(
            src_ref=lift.at[lax.rem(me + k, n)], dst_ref=lifted.at[slot], send_sem=l_send.at[k],
            recv_sem=l_recv.at[k], device_id=device(k, 0), device_id_type=MESH,
        )

    def send_lift(k, _):
        lift_copy(k, me).start()
        return 0

    lax.fori_loop(1, n, send_lift, 0)
    lifted[me] = lift[me]

    grow = (iota((LANES, cells), 0) % SG == iota((LANES, cells), 1) % SG).astype(jnp.float32)
    grown = jnp.dot(blocks, grow.astype(jnp.bfloat16), preferred_element_type=jnp.float32)
    lines = [
        jnp.sum(jnp.where(same, grown[i * SG : (i + 1) * SG], 0.0), 0, keepdims=True)
        for i in range(2 * SLOTS)
    ]
    res_ref[...] = jnp.concatenate(lines, 0).astype(jnp.bfloat16)

    def turn_chunk(k, one, two, spread):
        value = lifted[lax.rem(me + n - k, n)].astype(jnp.float32) * scale
        for h in range(HIGH):
            for r in range(0, ROWS, 2):
                by_cos = []
                by_sin = []
                for t in (r, r + 1):
                    re = value[t : t + 1]
                    im = value[ROWS + t : ROWS + t + 1]
                    by_cos.append(re * one[h] + im * two[h])
                    by_sin.append(re * two[h] - im * one[h])
                rows = pl.ds((h * ROWS + r) * 8, 16)
                spread[rows, 0:LANES] = jnp.concatenate(by_cos, 0).astype(jnp.bfloat16)
                spread[rows, LANES : 2 * LANES] = jnp.concatenate(by_sin, 0).astype(jnp.bfloat16)

    def gather(spread, low):
        term = lax.dot_general(
            spread[...], low[...], (((1,), (1,)), ((), ())), preferred_element_type=jnp.float32
        )
        for h in range(HIGH):
            out_ref[:, pl.ds(h * LOW, LOW)] += term[h * 8 * ROWS : (h + 1) * 8 * ROWS]

    def take_lift(k):
        lift_copy(k, lax.rem(me + n - k, n)).wait_recv()

    def grid(i, _):
        k = 2 * i
        take_lift(k + 1)
        low, one, two = odd(pairs - i - 1)
        gather(spread_even, low_even.at[pairs - i])
        turn_chunk(k + 1, one, two, spread_odd)
        pl.when(k + 2 < n)(lambda: take_lift(k + 2))
        gather(spread_odd, low)
        _, one, two = even(pairs - i - 1)
        turn_chunk(lax.rem(k + 2, n), one, two, spread_even)
        return 0

    out_ref[...] = jnp.zeros(out_ref.shape, jnp.float32)
    _, one, two = even(pairs)
    turn_chunk(0, one, two, spread_even)
    lax.fori_loop(0, pairs, grid, 0)

    def drain(k, _):
        v_copy(k, me).wait_send()
        lift_copy(k, me).wait_send()
        strip_copy(k, me).wait_send()
        return 0

    lax.fori_loop(1, n, drain, 0)
    for j in range(1, nf):
        model_copy(j, mf).wait_send()


def per_device(facets, observed, sub_u, sub_v, sub_block, sub_count, gain_real, gain_imag):
    n = lax.axis_size("base")
    nf = lax.axis_size("facet")
    assert facets.shape == (ROWS, COLS, 2, FS) and nf * COLS == NF and n % 2 == 0
    assert observed.shape == (SLOTS, 2, SG * SG)
    scale = 1.0 / math.sqrt(NF * n * ROWS * FS)
    hbm = pl.BlockSpec(memory_space=pltpu.HBM)
    vmem = pl.BlockSpec(memory_space=pltpu.VMEM)
    bf16 = jnp.bfloat16
    f32 = jnp.float32
    dma = pltpu.SemaphoreType.DMA
    out, res = pl.pallas_call(
        functools.partial(kernel, n, nf, scale),
        out_shape=(
            jax.ShapeDtypeStruct((ROWS * COLS * 2, FS), f32),
            jax.ShapeDtypeStruct((SLOTS * 2, SG * SG), bf16),
        ),
        in_specs=[hbm] * 8,
        out_specs=(vmem, vmem),
        scratch_shapes=[
            pltpu.SMEM((SLOTS,), jnp.int32),
            pltpu.SMEM((SLOTS,), jnp.int32),
            pltpu.SMEM((SLOTS,), jnp.int32),
            pltpu.SMEM((SLOTS,), jnp.int32),
            pltpu.SMEM(gain_real.shape, f32),
            pltpu.SMEM(gain_imag.shape, f32),
            pltpu.VMEM(observed.shape, bf16),
            pltpu.VMEM(facets.shape, bf16),
            pltpu.VMEM((ROWS * COLS * 2, FS), bf16),
            pltpu.VMEM((n, 8, LANES), jnp.int32),
            pltpu.VMEM((64, LANES), jnp.int32),
            pltpu.VMEM((64, LANES), jnp.int32),
            pltpu.VMEM((n // 2 + 1, LOW, 2 * LANES), bf16),
            pltpu.VMEM((n // 2, LOW, 2 * LANES), bf16),
            pltpu.VMEM((n // 2 + 1, HIGH, 8, LANES), f32),
            pltpu.VMEM((n // 2, HIGH, 8, LANES), f32),
            pltpu.VMEM((n // 2 + 1, HIGH, 8, LANES), f32),
            pltpu.VMEM((n // 2, HIGH, 8, LANES), f32),
            pltpu.VMEM((SLOTS * 2 * SG, n * 2 * ROWS), bf16),
            pltpu.VMEM((2 * SG, LANES), f32),
            pltpu.VMEM((HIGH * ROWS * 8, 2 * LANES), f32),
            pltpu.VMEM((HIGH * ROWS * 8, 2 * LANES), f32),
            pltpu.VMEM((n, 2 * ROWS, LANES), bf16),
            pltpu.VMEM((n, 2 * ROWS, LANES), bf16),
            pltpu.VMEM((nf, 2 * SG, LANES), bf16),
            pltpu.VMEM((n, 2 * ROWS, LANES), bf16),
            pltpu.VMEM((n, 2 * ROWS, LANES), bf16),
            pltpu.VMEM((HIGH * ROWS * 8, 2 * LANES), bf16),
            pltpu.VMEM((HIGH * ROWS * 8, 2 * LANES), bf16),
            dma((n,)), dma((n,)), dma((n,)), dma((n,)), dma((nf,)), dma((nf,)), dma((n,)), dma((n,)),
            dma((8,)),
        ],
        compiler_params=pltpu.CompilerParams(
            collective_id=0, has_side_effects=True, vmem_limit_bytes=62 * 1024 * 1024
        ),
    )(sub_v, sub_u, sub_block, sub_count, gain_real, gain_imag, observed, facets)
    return (out.reshape(ROWS, COLS, 2, FS), res.reshape(SLOTS, 2, SG * SG))


def solution(mesh):
    in_specs = (
        P("base", "facet", None, None),
        P("base", None, None),
        P("base"),
        P("base"),
        P("base"),
        P("base"),
        P(),
        P(),
    )
    out_specs = (P("base", "facet", None, None), P("base", None, None))
    return jax.shard_map(
        per_device, mesh=mesh, in_specs=in_specs, out_specs=out_specs, check_vma=False
    )
```

```python
import functools
import math

import jax
import jax.numpy as jnp
from jax import lax
from jax.experimental import pallas as pl
from jax.experimental.pallas import tpu as pltpu
from jax.sharding import PartitionSpec as P

FS = 4096
NPIX = 32768
SG = 32
NF = 16
CMAX = 4096
QUARTER = NPIX // 4
MESH = pl.DeviceIdType.MESH

LOW = 512
HIGH = FS // LOW
COLS = 4
ROWS = 8
SLOTS = 8
LANES = SLOTS * SG
HALF = LANES // 2
STEP = 16


def cos_turns(turns):
    away = jnp.abs(((turns + NPIX // 2) & (NPIX - 1)) - NPIX // 2)
    x = (QUARTER - away).astype(jnp.float32) * (2.0 * math.pi / NPIX)
    x2 = x * x
    tail = -1.0 / 39916800
    for term in (362880, -5040, 120, -6):
        tail = tail * x2 + 1.0 / term
    return x + x * (x2 * tail)


def iota(shape, dim):
    return lax.broadcasted_iota(jnp.int32, shape, dim)


def per_lane(values, shape):
    owner = iota(shape, len(shape) - 1) // SG
    out = jnp.full(shape, values[0])
    for s in range(1, SLOTS):
        out = jnp.where(owner == s, values[s], out)
    return out


def turned(one, two, c, s):
    return one * c + two * s, two * c - one * s


def phase_plan():
    shape = (64, LANES)
    group = iota(shape, 0) // 8
    line = iota(shape, 0) % 8
    facet = (line // 2 + 2) * FS
    shift = jnp.where(line == 0, 8, 64 << line)
    distance = jnp.where(group < 2, line, jnp.where(group < 4, line * STEP, facet))
    distance = jnp.where(group < 6, distance, shift)
    sine = (group == 1) | (group == 3) | (group == 7)
    quarter = jnp.where(group == 4, -(line % 2), jnp.where(group == 5, 1 - line % 2, 0))
    return distance, jnp.where(sine, -1, quarter) * QUARTER


def fill_tables(f, distance, quarter, low, one, two):
    table = cos_turns(jnp.concatenate([f] * 8, 0) * distance[...] + quarter[...])

    def by(i):
        return table[48 + i : 49 + i], table[56 + i : 57 + i]

    def add(pair, turn):
        return pair[0] * turn[0] - pair[1] * turn[1], pair[1] * turn[0] + pair[0] * turn[1]

    fine = (table[0:8], table[8:16])
    more = add(fine, by(0))
    fine = tuple(jnp.concatenate([x, y], 0) for x, y in zip(fine, more))
    steps = [(table[16:24], table[24:32])]
    steps.append(add(steps[0], by(1)))
    steps += [add(step, by(2)) for step in steps[:2]]
    lines = [(table[32:40], table[40:48])]
    for i in range(3):
        lines += [turned(*line, *by(3 + i)) for line in lines]
    for h in range(HIGH):
        one[h] = lines[h][0]
        two[h] = lines[h][1]
    for i in range(LOW // STEP):
        step = tuple(x[i % 8 : i % 8 + 1] for x in steps[i // 8])
        cos, sin = add(fine, step)
        rows = pl.ds(i * STEP, STEP)
        low[rows, 0:LANES] = cos.astype(jnp.bfloat16)
        low[rows, LANES : 2 * LANES] = sin.astype(jnp.bfloat16)


def kernel(
    n, nf, scale,
    v_raw, u_raw, block_raw, count_raw, gain_re_raw, gain_im_raw, seen_raw, facet_raw,
    out_ref, res_ref,
    v_ref, u_ref, block_ref, count_ref, gain_re_ref, gain_im_ref, seen_ref, facet_four,
    facet_ref, freq, distance, quarter, low, one, two, row_table,
    seen_cells, product, strip_out, strip, model, blocks, lift, lifted, spread, image,
    v_send, v_recv, s_send, s_recv, m_send, m_recv, l_send, l_recv, in_sem,
):
    me = lax.axis_index("base")
    mf = lax.axis_index("facet")
    pairs = n // 2

    def device(k, j):
        return {"base": lax.rem(me + k, n), "facet": lax.rem(mf + j, nf)}

    raw = [v_raw, facet_raw, seen_raw, u_raw, block_raw, count_raw, gain_re_raw, gain_im_raw]
    held = [v_ref, facet_four, seen_ref, u_ref, block_ref, count_ref, gain_re_ref, gain_im_ref]
    loads = [
        pltpu.make_async_copy(src, dst, in_sem.at[i]) for i, (src, dst) in enumerate(zip(raw, held))
    ]
    for load in loads:
        load.start()

    barrier = pltpu.get_barrier_semaphore()

    def greet(k, _):
        pl.semaphore_signal(barrier, inc=1, device_id=device(k, 0), device_id_type=MESH)
        return 0

    lax.fori_loop(1, n, greet, 0)
    for j in range(1, nf):
        pl.semaphore_signal(barrier, inc=1, device_id=device(0, j), device_id_type=MESH)

    loads[0].wait()
    freq[me] = per_lane([v_ref[s] for s in range(SLOTS)], (8, LANES)) + iota((8, LANES), 1) % SG
    distance[...], quarter[...] = phase_plan()

    loads[1].wait()
    for r in range(0, ROWS, 2):
        both = []
        for t in (r, r + 1):
            both += [facet_four[t, b].astype(jnp.float32) for b in range(COLS)]
        facet_ref[pl.ds(r * 8, 16), :] = jnp.concatenate(both, 0).astype(jnp.bfloat16)

    pl.semaphore_wait(barrier, n - 1 + nf - 1)

    def v_copy(k, slot):
        return pltpu.make_async_remote_copy(
            src_ref=freq.at[me], dst_ref=freq.at[slot], send_sem=v_send.at[k],
            recv_sem=v_recv.at[k], device_id=device(k, 0), device_id_type=MESH,
        )

    def send_v(k, _):
        v_copy(k, me).start()
        return 0

    lax.fori_loop(1, n, send_v, 0)

    for load in loads[2:]:
        load.wait()

    wide = n * 2 * ROWS
    lane = iota((2 * SG, wide), 1)
    sub = iota((2 * SG, wide), 0)
    turn = (sub // SG - lane // ROWS % 2) * QUARTER
    first = (FS - n * ROWS) // 2 + lane // (2 * ROWS) * ROWS + lane % ROWS

    place = first + (mf + 2) * FS

    def fill_rows(s, _):
        row_table[pl.ds(pl.multiple_of(s * 2 * SG, 2 * SG), 2 * SG), :] = cos_turns(
            (sub % SG + u_ref[s]) * place + turn
        ).astype(jnp.bfloat16)
        return 0

    lax.fori_loop(0, SLOTS, fill_rows, 0)

    group = iota((2 * SG, LANES), 1) // SG
    cells = SG * SG
    same = iota((SG, cells), 1) // SG == iota((SG, cells), 0)
    tall = []
    for s in range(SLOTS):
        seen = seen_ref[s].astype(jnp.float32)
        tall += [jnp.where(same, seen[i : i + 1], 0.0).astype(jnp.bfloat16) for i in range(2)]
    tall = jnp.concatenate(tall, 0)
    pick = (iota((cells, LANES), 0) % SG == iota((cells, LANES), 1) % SG).astype(jnp.float32)
    picked = jnp.dot(tall, pick.astype(jnp.bfloat16), preferred_element_type=jnp.float32)
    placed = jnp.zeros((2 * SG, LANES), jnp.float32)
    for s in range(SLOTS):
        placed = jnp.where(group == s, picked[s * 2 * SG : (s + 1) * 2 * SG], placed)
    seen_cells[...] = placed

    def strip_copy(half, k, slot):
        return pltpu.make_async_remote_copy(
            src_ref=strip_out.at[half, k], dst_ref=strip.at[half, slot],
            send_sem=s_send.at[half, k], recv_sem=s_recv.at[half, k], device_id=device(k, 0),
            device_id_type=MESH,
        )

    def model_copy(half, j, slot):
        return pltpu.make_async_remote_copy(
            src_ref=model.at[half, mf], dst_ref=model.at[half, slot],
            send_sem=m_send.at[half, j], recv_sem=m_recv.at[half, j], device_id=device(0, j),
            device_id_type=MESH,
        )

    def lift_copy(half, k, slot):
        return pltpu.make_async_remote_copy(
            src_ref=lift.at[half, lax.rem(me + k, n)], dst_ref=lifted.at[half, slot],
            send_sem=l_send.at[half, k], recv_sem=l_recv.at[half, k], device_id=device(k, 0),
            device_id_type=MESH,
        )

    def take_v(k):
        v_copy(n - k, lax.rem(me + k, n)).wait_recv()

    def degrid(half, i):
        k = 2 * i
        g = lax.rem(me + k, n)
        g_next = lax.rem(me + k + 1, n)
        if half == 0:
            pl.when(k > 0)(lambda: take_v(k))
            take_v(k + 1)
        at = half * pairs + i
        part = slice(half * HALF, (half + 1) * HALF)
        f = jnp.concatenate([freq[g][:, part], freq[g_next][:, part]], 1)
        fill_tables(f, distance, quarter, low.at[at], one.at[at], two.at[at])
        tall = jnp.concatenate([facet_ref[:, h * LOW : (h + 1) * LOW] for h in range(HIGH)], 0)
        product[...] = jnp.dot(tall, low[at], preferred_element_type=jnp.float32)
        lines_re = []
        lines_im = []
        for r in range(ROWS):
            total_re = jnp.zeros((8, LANES), jnp.float32)
            total_im = jnp.zeros((8, LANES), jnp.float32)
            for h in range(HIGH):
                rows = pl.ds((h * ROWS + r) * 8, 8)
                part_cos = product[rows, 0:LANES]
                part_sin = product[rows, LANES : 2 * LANES]
                total_re = total_re + (part_cos * one[at, h] + part_sin * two[at, h])
                total_im = total_im + (part_cos * two[at, h] - part_sin * one[at, h])
            lines_re.append(jnp.sum(total_re, 0, keepdims=True))
            lines_im.append(jnp.sum(total_im, 0, keepdims=True))
        chunk = jnp.concatenate(lines_re + lines_im, 0).astype(jnp.bfloat16)
        strip_out[half, k] = chunk[:, :HALF]
        strip_out[half, k + 1] = chunk[:, HALF:]

        @pl.when(k == 0)
        def _():
            strip[half, me] = strip_out[half, 0]

        @pl.when(k > 0)
        def _():
            strip_copy(half, k, me).start()

        strip_copy(half, k + 1, me).start()

    half_rows = SLOTS // 2 * 2 * SG
    owner = iota((2 * SG, HALF), 1) // SG

    def sum_rows(half):
        def take(k, _):
            strip_copy(half, k, lax.rem(me + n - k, n)).wait_recv()
            return 0

        lax.fori_loop(1, n, take, 0)
        crossed = jnp.dot(
            row_table[half * half_rows : (half + 1) * half_rows, :],
            strip[half].reshape(wide, HALF),
            preferred_element_type=jnp.float32,
        )
        part = jnp.zeros((2 * SG, HALF), jnp.float32)
        for s in range(SLOTS // 2):
            part = jnp.where(owner == s, crossed[s * 2 * SG : (s + 1) * 2 * SG], part)
        model[half, mf] = (part * scale).astype(jnp.bfloat16)
        for j in range(1, nf):
            model_copy(half, j, mf).start()

    def raise_rows(half):
        full = (SG, LANES)
        part = slice(half * HALF, (half + 1) * HALF)
        gain_re = per_lane([gain_re_ref[block_ref[s]] for s in range(SLOTS)], full)[:, part]
        gain_im = per_lane([gain_im_ref[block_ref[s]] for s in range(SLOTS)], full)[:, part]
        weight = per_lane([count_ref[s] for s in range(SLOTS)], full)[:, part]
        weight = weight.astype(jnp.float32) / CMAX
        seen = seen_cells[:, part]
        for j in range(1, nf):
            model_copy(half, j, lax.rem(mf + nf - j, nf)).wait_recv()
        whole = model[half, 0].astype(jnp.float32)
        for j in range(1, nf):
            whole = whole + model[half, j].astype(jnp.float32)
        model_re = whole[:SG]
        model_im = whole[SG:]
        diff_re = seen[:SG] - (gain_re * model_re - gain_im * model_im)
        diff_im = seen[SG:] - (gain_re * model_im + gain_im * model_re)
        res_re = weight * (gain_re * diff_re + gain_im * diff_im)
        res_im = weight * (gain_re * diff_im - gain_im * diff_re)
        residual = jnp.concatenate([res_re, res_im], 0)
        blocks[half] = jnp.concatenate(
            [
                jnp.where(owner == s, residual, 0.0).astype(jnp.bfloat16)
                for s in range(SLOTS // 2)
            ],
            0,
        )
        raised = lax.dot_general(
            row_table[half * half_rows : (half + 1) * half_rows, :],
            blocks[half],
            (((0,), (0,)), ((), ())),
            preferred_element_type=jnp.float32,
        )
        lift[half] = raised.astype(jnp.bfloat16).reshape(n, 2 * ROWS, HALF)

        def send(k, _):
            lift_copy(half, k, me).start()
            return 0

        lax.fori_loop(1, n, send, 0)
        lifted[half, me] = lift[half, me]

    def grid(half, i):
        k = 2 * i
        g = lax.rem(me + k, n)
        g_next = lax.rem(me + k + 1, n)
        pl.when(k > 0)(lambda: lift_copy(half, n - k, g).wait_recv())
        lift_copy(half, n - k - 1, g_next).wait_recv()
        at = half * pairs + i
        value = jnp.concatenate([lifted[half, g], lifted[half, g_next]], 1)
        value = value.astype(jnp.float32) * scale
        for h in range(HIGH):
            for r in range(0, ROWS, 2):
                by_cos = []
                by_sin = []
                for t in (r, r + 1):
                    re = value[t : t + 1]
                    im = value[ROWS + t : ROWS + t + 1]
                    by_cos.append(re * one[at, h] + im * two[at, h])
                    by_sin.append(re * two[at, h] - im * one[at, h])
                rows = pl.ds((h * ROWS + r) * 8, 16)
                spread[rows, 0:LANES] = jnp.concatenate(by_cos, 0).astype(jnp.bfloat16)
                spread[rows, LANES : 2 * LANES] = jnp.concatenate(by_sin, 0).astype(jnp.bfloat16)
        term = lax.dot_general(
            spread[...], low[at], (((1,), (1,)), ((), ())), preferred_element_type=jnp.float32
        )
        for h in range(HIGH):
            image[:, pl.ds(h * LOW, LOW)] += term[h * 8 * ROWS : (h + 1) * 8 * ROWS]

    def loop(first, last, step, half):
        def body(i, _):
            step(half, i)
            return 0

        lax.fori_loop(first, last, body, 0)

    middle = (pairs + 1) // 2
    loop(0, pairs, degrid, 0)
    loop(0, middle, degrid, 1)
    sum_rows(0)
    loop(middle, pairs, degrid, 1)
    raise_rows(0)
    sum_rows(1)
    image[...] = jnp.zeros(image.shape, jnp.float32)
    loop(0, middle, grid, 0)
    raise_rows(1)
    loop(middle, pairs, grid, 0)

    grow = (iota((HALF, cells), 0) % SG == iota((HALF, cells), 1) % SG).astype(jnp.float32)
    grown = jnp.dot(
        blocks[...].reshape(2 * half_rows, HALF),
        grow.astype(jnp.bfloat16),
        preferred_element_type=jnp.float32,
    )
    for s in range(SLOTS):
        lines = [
            jnp.sum(jnp.where(same, grown[i * SG : (i + 1) * SG], 0.0), 0, keepdims=True)
            for i in (2 * s, 2 * s + 1)
        ]
        res_ref[s] = jnp.concatenate(lines, 0).astype(jnp.bfloat16)

    loop(0, pairs, grid, 1)
    for r in range(ROWS):
        for b in range(COLS):
            line = r * 8 + b * 2
            out_ref[r, b] = image[line : line + 2, :]

    def drain(k, _):
        v_copy(k, me).wait_send()
        for half in range(2):
            strip_copy(half, k, me).wait_send()
            lift_copy(half, k, me).wait_send()
        return 0

    lax.fori_loop(1, n, drain, 0)
    for half in range(2):
        for j in range(1, nf):
            model_copy(half, j, mf).wait_send()


def per_device(facets, observed, sub_u, sub_v, sub_block, sub_count, gain_real, gain_imag):
    n = lax.axis_size("base")
    nf = lax.axis_size("facet")
    assert facets.shape == (ROWS, COLS, 2, FS) and nf * COLS == NF and n % 2 == 0
    assert observed.shape == (SLOTS, 2, SG * SG)
    scale = 1.0 / math.sqrt(NF * n * ROWS * FS)
    hbm = pl.BlockSpec(memory_space=pltpu.HBM)
    vmem = pl.BlockSpec(memory_space=pltpu.VMEM)
    bf16 = jnp.bfloat16
    f32 = jnp.float32
    dma = pltpu.SemaphoreType.DMA
    return pl.pallas_call(
        functools.partial(kernel, n, nf, scale),
        out_shape=(
            jax.ShapeDtypeStruct(facets.shape, f32),
            jax.ShapeDtypeStruct(observed.shape, bf16),
        ),
        in_specs=[hbm] * 8,
        out_specs=(vmem, vmem),
        scratch_shapes=[
            pltpu.SMEM((SLOTS,), jnp.int32),
            pltpu.SMEM((SLOTS,), jnp.int32),
            pltpu.SMEM((SLOTS,), jnp.int32),
            pltpu.SMEM((SLOTS,), jnp.int32),
            pltpu.SMEM(gain_real.shape, f32),
            pltpu.SMEM(gain_imag.shape, f32),
            pltpu.VMEM(observed.shape, bf16),
            pltpu.VMEM(facets.shape, bf16),
            pltpu.VMEM((ROWS * COLS * 2, FS), bf16),
            pltpu.VMEM((n, 8, LANES), jnp.int32),
            pltpu.VMEM((64, LANES), jnp.int32),
            pltpu.VMEM((64, LANES), jnp.int32),
            pltpu.VMEM((n, LOW, 2 * LANES), bf16),
            pltpu.VMEM((n, HIGH, 8, LANES), f32),
            pltpu.VMEM((n, HIGH, 8, LANES), f32),
            pltpu.VMEM((SLOTS * 2 * SG, n * 2 * ROWS), bf16),
            pltpu.VMEM((2 * SG, LANES), f32),
            pltpu.VMEM((HIGH * ROWS * 8, 2 * LANES), f32),
            pltpu.VMEM((2, n, 2 * ROWS, HALF), bf16),
            pltpu.VMEM((2, n, 2 * ROWS, HALF), bf16),
            pltpu.VMEM((2, nf, 2 * SG, HALF), bf16),
            pltpu.VMEM((2, SLOTS // 2 * 2 * SG, HALF), bf16),
            pltpu.VMEM((2, n, 2 * ROWS, HALF), bf16),
            pltpu.VMEM((2, n, 2 * ROWS, HALF), bf16),
            pltpu.VMEM((HIGH * ROWS * 8, 2 * LANES), bf16),
            pltpu.VMEM((ROWS * COLS * 2, FS), f32),
            dma((n,)), dma((n,)), dma((2, n)), dma((2, n)), dma((2, nf)), dma((2, nf)),
            dma((2, n)), dma((2, n)), dma((8,)),
        ],
        compiler_params=pltpu.CompilerParams(
            collective_id=0, has_side_effects=True, vmem_limit_bytes=62 * 1024 * 1024
        ),
    )(sub_v, sub_u, sub_block, sub_count, gain_real, gain_imag, observed, facets)


def solution(mesh):
    in_specs = (
        P("base", "facet", None, None),
        P("base", None, None),
        P("base"),
        P("base"),
        P("base"),
        P("base"),
        P(),
        P(),
    )
    out_specs = (P("base", "facet", None, None), P("base", None, None))
    return jax.shard_map(
        per_device, mesh=mesh, in_specs=in_specs, out_specs=out_specs, check_vma=False
    )
```

```python
import functools
import math

import jax
import jax.numpy as jnp
from jax import lax
from jax.experimental import pallas as pl
from jax.experimental.pallas import tpu as pltpu
from jax.sharding import PartitionSpec as P

FS = 4096
NPIX = 32768
SG = 32
NF = 16
CMAX = 4096
QUARTER = NPIX // 4
MESH = pl.DeviceIdType.MESH

LOW = 512
SIDE = LOW // 2
HIGH = FS // LOW
COLS = 4
ROWS = 8
SLOTS = 8
LANES = SLOTS * SG
HALF = LANES // 2
STEP = 16


def cos_turns(turns, period=NPIX):
    away = jnp.abs(((turns + period // 2) & (period - 1)) - period // 2)
    x = (period // 4 - away).astype(jnp.float32) * (2.0 * math.pi / period)
    x2 = x * x
    tail = -1.0 / 39916800
    for term in (362880, -5040, 120, -6):
        tail = tail * x2 + 1.0 / term
    return x + x * (x2 * tail)


def iota(shape, dim):
    return lax.broadcasted_iota(jnp.int32, shape, dim)


def per_lane(values, shape):
    owner = iota(shape, len(shape) - 1) // SG
    out = jnp.full(shape, values[0])
    for s in range(1, SLOTS):
        out = jnp.where(owner == s, values[s], out)
    return out


def turned(one, two, c, s):
    return one * c + two * s, two * c - one * s


def phase_plan():
    shape = (64, LANES)
    group = iota(shape, 0) // 8
    line = iota(shape, 0) % 8
    facet = (line // 2 + 2) * 2 * FS + LOW - 1
    shift = jnp.where(line == 0, STEP, jnp.where(line == 1, STEP * STEP, LOW // 2 << line))
    distance = jnp.where(group < 2, 2 * line + 1, jnp.where(group < 4, line * 2 * STEP, facet))
    distance = jnp.where(group < 6, distance, shift)
    sine = (group == 1) | (group == 3) | (group == 7)
    quarter = jnp.where(group == 4, -(line % 2), jnp.where(group == 5, 1 - line % 2, 0))
    return distance, jnp.where(sine, -1, quarter) * 2 * QUARTER


def fill_tables(f, distance, quarter, low, one, two):
    table = cos_turns(jnp.concatenate([f] * 8, 0) * distance[...] + quarter[...], 2 * NPIX)

    def by(i):
        return table[48 + i : 49 + i], table[56 + i : 57 + i]

    def add(pair, turn):
        return pair[0] * turn[0] - pair[1] * turn[1], pair[1] * turn[0] + pair[0] * turn[1]

    fine = (table[0:8], table[8:16])
    more = add(fine, by(0))
    fine = tuple(jnp.concatenate([x, y], 0) for x, y in zip(fine, more))
    steps = [(table[16:24], table[24:32])]
    steps.append(add(steps[0], by(1)))
    lines = [(table[32:40], table[40:48])]
    for i in range(3):
        lines += [turned(*line, *by(2 + i)) for line in lines]
    for h in range(HIGH):
        one[h] = lines[h][0]
        two[h] = lines[h][1]
    for i in range(SIDE // STEP):
        step = tuple(x[i % 8 : i % 8 + 1] for x in steps[i // 8])
        cos, sin = add(fine, step)
        rows = pl.ds(i * STEP, STEP)
        low[rows, 0:LANES] = cos.astype(jnp.bfloat16)
        low[rows, LANES : 2 * LANES] = sin.astype(jnp.bfloat16)


def kernel(
    n, nf, scale,
    v_raw, u_raw, block_raw, count_raw, gain_re_raw, gain_im_raw, seen_raw, facet_raw,
    out_ref, res_ref,
    v_ref, u_ref, block_ref, count_ref, gain_re_ref, gain_im_ref, seen_ref, facet_four,
    facet_ref, plus, minus, freq, distance, quarter, low, one, two, row_table,
    seen_cells, product, strip_out, strip, model, blocks, lift, lifted, spread, image,
    v_send, v_recv, s_send, s_recv, m_send, m_recv, l_send, l_recv, in_sem,
):
    me = lax.axis_index("base")
    mf = lax.axis_index("facet")
    pairs = n // 2

    def device(k, j):
        return {"base": lax.rem(me + k, n), "facet": lax.rem(mf + j, nf)}

    raw = [v_raw, facet_raw, seen_raw, u_raw, block_raw, count_raw, gain_re_raw, gain_im_raw]
    held = [v_ref, facet_four, seen_ref, u_ref, block_ref, count_ref, gain_re_ref, gain_im_ref]
    loads = [
        pltpu.make_async_copy(src, dst, in_sem.at[i]) for i, (src, dst) in enumerate(zip(raw, held))
    ]
    for load in loads:
        load.start()

    barrier = pltpu.get_barrier_semaphore()

    def greet(k, _):
        pl.semaphore_signal(barrier, inc=1, device_id=device(k, 0), device_id_type=MESH)
        return 0

    lax.fori_loop(1, n, greet, 0)
    for j in range(1, nf):
        pl.semaphore_signal(barrier, inc=1, device_id=device(0, j), device_id_type=MESH)

    loads[0].wait()
    freq[me] = per_lane([v_ref[s] for s in range(SLOTS)], (8, LANES)) + iota((8, LANES), 1) % SG
    distance[...], quarter[...] = phase_plan()

    loads[1].wait()
    for r in range(0, ROWS, 2):
        both = []
        for t in (r, r + 1):
            both += [facet_four[t, b].astype(jnp.float32) for b in range(COLS)]
        facet_ref[pl.ds(r * 8, 16), :] = jnp.concatenate(both, 0).astype(jnp.bfloat16)
    flip = (iota((SIDE, SIDE), 0) + iota((SIDE, SIDE), 1) == SIDE - 1).astype(jnp.float32)
    left = [facet_ref[:, h * LOW : h * LOW + SIDE] for h in range(HIGH)]
    right = [facet_ref[:, h * LOW + SIDE : (h + 1) * LOW] for h in range(HIGH)]
    left = jnp.dot(
        jnp.concatenate(left, 0), flip.astype(jnp.bfloat16), preferred_element_type=jnp.float32
    )
    right = jnp.concatenate(right, 0).astype(jnp.float32)
    plus[...] = (right + left).astype(jnp.bfloat16)
    minus[...] = (right - left).astype(jnp.bfloat16)

    pl.semaphore_wait(barrier, n - 1 + nf - 1)

    def v_copy(k, slot):
        return pltpu.make_async_remote_copy(
            src_ref=freq.at[me], dst_ref=freq.at[slot], send_sem=v_send.at[k],
            recv_sem=v_recv.at[k], device_id=device(k, 0), device_id_type=MESH,
        )

    def send_v(k, _):
        v_copy(k, me).start()
        return 0

    lax.fori_loop(1, n, send_v, 0)

    for load in loads[2:]:
        load.wait()

    wide = n * 2 * ROWS
    lane = iota((2 * SG, wide), 1)
    sub = iota((2 * SG, wide), 0)
    turn = (sub // SG - lane // ROWS % 2) * QUARTER
    first = (FS - n * ROWS) // 2 + lane // (2 * ROWS) * ROWS + lane % ROWS

    place = first + (mf + 2) * FS

    def fill_rows(s, _):
        row_table[pl.ds(pl.multiple_of(s * 2 * SG, 2 * SG), 2 * SG), :] = cos_turns(
            (sub % SG + u_ref[s]) * place + turn
        ).astype(jnp.bfloat16)
        return 0

    lax.fori_loop(0, SLOTS, fill_rows, 0)

    group = iota((2 * SG, LANES), 1) // SG
    cells = SG * SG
    same = iota((SG, cells), 1) // SG == iota((SG, cells), 0)
    tall = []
    for s in range(SLOTS):
        seen = seen_ref[s].astype(jnp.float32)
        tall += [jnp.where(same, seen[i : i + 1], 0.0).astype(jnp.bfloat16) for i in range(2)]
    tall = jnp.concatenate(tall, 0)
    pick = (iota((cells, LANES), 0) % SG == iota((cells, LANES), 1) % SG).astype(jnp.float32)
    picked = jnp.dot(tall, pick.astype(jnp.bfloat16), preferred_element_type=jnp.float32)
    placed = jnp.zeros((2 * SG, LANES), jnp.float32)
    for s in range(SLOTS):
        placed = jnp.where(group == s, picked[s * 2 * SG : (s + 1) * 2 * SG], placed)
    seen_cells[...] = placed

    def strip_copy(half, k, slot):
        return pltpu.make_async_remote_copy(
            src_ref=strip_out.at[half, k], dst_ref=strip.at[half, slot],
            send_sem=s_send.at[half, k], recv_sem=s_recv.at[half, k], device_id=device(k, 0),
            device_id_type=MESH,
        )

    def model_copy(half, j, slot):
        return pltpu.make_async_remote_copy(
            src_ref=model.at[half, mf], dst_ref=model.at[half, slot],
            send_sem=m_send.at[half, j], recv_sem=m_recv.at[half, j], device_id=device(0, j),
            device_id_type=MESH,
        )

    def lift_copy(half, k, slot):
        return pltpu.make_async_remote_copy(
            src_ref=lift.at[half, lax.rem(me + k, n)], dst_ref=lifted.at[half, slot],
            send_sem=l_send.at[half, k], recv_sem=l_recv.at[half, k], device_id=device(k, 0),
            device_id_type=MESH,
        )

    def take_v(k):
        v_copy(n - k, lax.rem(me + k, n)).wait_recv()

    def degrid(half, i):
        k = 2 * i
        g = lax.rem(me + k, n)
        g_next = lax.rem(me + k + 1, n)
        if half == 0:
            pl.when(k > 0)(lambda: take_v(k))
            take_v(k + 1)
        at = half * pairs + i
        part = slice(half * HALF, (half + 1) * HALF)
        f = jnp.concatenate([freq[g][:, part], freq[g_next][:, part]], 1)
        fill_tables(f, distance, quarter, low.at[at], one.at[at], two.at[at])
        product[:, :LANES] = jnp.dot(
            plus[...], low[at, :, :LANES], preferred_element_type=jnp.float32
        )
        product[:, LANES:] = jnp.dot(
            minus[...], low[at, :, LANES:], preferred_element_type=jnp.float32
        )
        lines_re = []
        lines_im = []
        for r in range(ROWS):
            total_re = jnp.zeros((8, LANES), jnp.float32)
            total_im = jnp.zeros((8, LANES), jnp.float32)
            for h in range(HIGH):
                rows = pl.ds((h * ROWS + r) * 8, 8)
                part_cos = product[rows, 0:LANES]
                part_sin = product[rows, LANES : 2 * LANES]
                total_re = total_re + (part_cos * one[at, h] + part_sin * two[at, h])
                total_im = total_im + (part_cos * two[at, h] - part_sin * one[at, h])
            lines_re.append(jnp.sum(total_re, 0, keepdims=True))
            lines_im.append(jnp.sum(total_im, 0, keepdims=True))
        chunk = jnp.concatenate(lines_re + lines_im, 0).astype(jnp.bfloat16)
        strip_out[half, k] = chunk[:, :HALF]
        strip_out[half, k + 1] = chunk[:, HALF:]

        @pl.when(k == 0)
        def _():
            strip[half, me] = strip_out[half, 0]

        @pl.when(k > 0)
        def _():
            strip_copy(half, k, me).start()

        strip_copy(half, k + 1, me).start()

    half_rows = SLOTS // 2 * 2 * SG
    owner = iota((2 * SG, HALF), 1) // SG

    def sum_rows(half):
        def take(k, _):
            strip_copy(half, k, lax.rem(me + n - k, n)).wait_recv()
            return 0

        lax.fori_loop(1, n, take, 0)
        crossed = jnp.dot(
            row_table[half * half_rows : (half + 1) * half_rows, :],
            strip[half].reshape(wide, HALF),
            preferred_element_type=jnp.float32,
        )
        part = jnp.zeros((2 * SG, HALF), jnp.float32)
        for s in range(SLOTS // 2):
            part = jnp.where(owner == s, crossed[s * 2 * SG : (s + 1) * 2 * SG], part)
        model[half, mf] = (part * scale).astype(jnp.bfloat16)
        for j in range(1, nf):
            model_copy(half, j, mf).start()

    def raise_rows(half):
        full = (SG, LANES)
        part = slice(half * HALF, (half + 1) * HALF)
        gain_re = per_lane([gain_re_ref[block_ref[s]] for s in range(SLOTS)], full)[:, part]
        gain_im = per_lane([gain_im_ref[block_ref[s]] for s in range(SLOTS)], full)[:, part]
        weight = per_lane([count_ref[s] for s in range(SLOTS)], full)[:, part]
        weight = weight.astype(jnp.float32) / CMAX
        seen = seen_cells[:, part]
        for j in range(1, nf):
            model_copy(half, j, lax.rem(mf + nf - j, nf)).wait_recv()
        whole = model[half, 0].astype(jnp.float32)
        for j in range(1, nf):
            whole = whole + model[half, j].astype(jnp.float32)
        model_re = whole[:SG]
        model_im = whole[SG:]
        diff_re = seen[:SG] - (gain_re * model_re - gain_im * model_im)
        diff_im = seen[SG:] - (gain_re * model_im + gain_im * model_re)
        res_re = weight * (gain_re * diff_re + gain_im * diff_im)
        res_im = weight * (gain_re * diff_im - gain_im * diff_re)
        residual = jnp.concatenate([res_re, res_im], 0)
        blocks[half] = jnp.concatenate(
            [
                jnp.where(owner == s, residual, 0.0).astype(jnp.bfloat16)
                for s in range(SLOTS // 2)
            ],
            0,
        )
        raised = lax.dot_general(
            row_table[half * half_rows : (half + 1) * half_rows, :],
            blocks[half],
            (((0,), (0,)), ((), ())),
            preferred_element_type=jnp.float32,
        )
        lift[half] = raised.astype(jnp.bfloat16).reshape(n, 2 * ROWS, HALF)

        def send(k, _):
            lift_copy(half, k, me).start()
            return 0

        lax.fori_loop(1, n, send, 0)
        lifted[half, me] = lift[half, me]

    def grid(half, i):
        k = 2 * i
        g = lax.rem(me + k, n)
        g_next = lax.rem(me + k + 1, n)
        pl.when(k > 0)(lambda: lift_copy(half, n - k, g).wait_recv())
        lift_copy(half, n - k - 1, g_next).wait_recv()
        at = half * pairs + i
        value = jnp.concatenate([lifted[half, g], lifted[half, g_next]], 1)
        value = value.astype(jnp.float32) * scale
        for h in range(HIGH):
            for r in range(0, ROWS, 2):
                by_cos = []
                by_sin = []
                for t in (r, r + 1):
                    re = value[t : t + 1]
                    im = value[ROWS + t : ROWS + t + 1]
                    by_cos.append(re * one[at, h] + im * two[at, h])
                    by_sin.append(re * two[at, h] - im * one[at, h])
                rows = pl.ds((h * ROWS + r) * 8, 16)
                spread[rows, 0:LANES] = jnp.concatenate(by_cos, 0).astype(jnp.bfloat16)
                spread[rows, LANES : 2 * LANES] = jnp.concatenate(by_sin, 0).astype(jnp.bfloat16)
        for p in range(2):
            lanes = slice(p * LANES, (p + 1) * LANES)
            image[p] += lax.dot_general(
                spread[:, lanes],
                low[at, :, lanes],
                (((1,), (1,)), ((), ())),
                preferred_element_type=jnp.float32,
            )

    def loop(first, last, step, half):
        def body(i, _):
            step(half, i)
            return 0

        lax.fori_loop(first, last, body, 0)

    middle = (pairs + 1) // 2
    loop(0, pairs, degrid, 0)
    loop(0, middle, degrid, 1)
    sum_rows(0)
    loop(middle, pairs, degrid, 1)
    raise_rows(0)
    sum_rows(1)
    image[...] = jnp.zeros(image.shape, jnp.float32)
    loop(0, middle, grid, 0)
    raise_rows(1)
    loop(middle, pairs, grid, 0)

    grow = (iota((HALF, cells), 0) % SG == iota((HALF, cells), 1) % SG).astype(jnp.float32)
    grown = jnp.dot(
        blocks[...].reshape(2 * half_rows, HALF),
        grow.astype(jnp.bfloat16),
        preferred_element_type=jnp.float32,
    )
    for s in range(SLOTS):
        lines = [
            jnp.sum(jnp.where(same, grown[i * SG : (i + 1) * SG], 0.0), 0, keepdims=True)
            for i in (2 * s, 2 * s + 1)
        ]
        res_ref[s] = jnp.concatenate(lines, 0).astype(jnp.bfloat16)

    loop(0, pairs, grid, 1)
    right = image[0] + image[1]
    left = jnp.dot(
        image[0] - image[1],
        flip,
        preferred_element_type=jnp.float32,
        precision=lax.Precision.HIGHEST,
    )
    for h in range(HIGH):
        rows = slice(h * 8 * ROWS, (h + 1) * 8 * ROWS)
        both = jnp.concatenate([left[rows], right[rows]], 1)
        for r in range(ROWS):
            for b in range(COLS):
                line = r * 8 + b * 2
                out_ref[r, b, :, h * LOW : (h + 1) * LOW] = both[line : line + 2]

    def drain(k, _):
        v_copy(k, me).wait_send()
        for half in range(2):
            strip_copy(half, k, me).wait_send()
            lift_copy(half, k, me).wait_send()
        return 0

    lax.fori_loop(1, n, drain, 0)
    for half in range(2):
        for j in range(1, nf):
            model_copy(half, j, mf).wait_send()


def per_device(facets, observed, sub_u, sub_v, sub_block, sub_count, gain_real, gain_imag):
    n = lax.axis_size("base")
    nf = lax.axis_size("facet")
    assert facets.shape == (ROWS, COLS, 2, FS) and nf * COLS == NF and n % 2 == 0
    assert observed.shape == (SLOTS, 2, SG * SG)
    scale = 1.0 / math.sqrt(NF * n * ROWS * FS)
    hbm = pl.BlockSpec(memory_space=pltpu.HBM)
    vmem = pl.BlockSpec(memory_space=pltpu.VMEM)
    bf16 = jnp.bfloat16
    f32 = jnp.float32
    dma = pltpu.SemaphoreType.DMA
    return pl.pallas_call(
        functools.partial(kernel, n, nf, scale),
        out_shape=(
            jax.ShapeDtypeStruct(facets.shape, f32),
            jax.ShapeDtypeStruct(observed.shape, bf16),
        ),
        in_specs=[hbm] * 8,
        out_specs=(vmem, vmem),
        scratch_shapes=[
            pltpu.SMEM((SLOTS,), jnp.int32),
            pltpu.SMEM((SLOTS,), jnp.int32),
            pltpu.SMEM((SLOTS,), jnp.int32),
            pltpu.SMEM((SLOTS,), jnp.int32),
            pltpu.SMEM(gain_real.shape, f32),
            pltpu.SMEM(gain_imag.shape, f32),
            pltpu.VMEM(observed.shape, bf16),
            pltpu.VMEM(facets.shape, bf16),
            pltpu.VMEM((ROWS * COLS * 2, FS), bf16),
            pltpu.VMEM((HIGH * ROWS * 8, SIDE), bf16),
            pltpu.VMEM((HIGH * ROWS * 8, SIDE), bf16),
            pltpu.VMEM((n, 8, LANES), jnp.int32),
            pltpu.VMEM((64, LANES), jnp.int32),
            pltpu.VMEM((64, LANES), jnp.int32),
            pltpu.VMEM((n, SIDE, 2 * LANES), bf16),
            pltpu.VMEM((n, HIGH, 8, LANES), f32),
            pltpu.VMEM((n, HIGH, 8, LANES), f32),
            pltpu.VMEM((SLOTS * 2 * SG, n * 2 * ROWS), bf16),
            pltpu.VMEM((2 * SG, LANES), f32),
            pltpu.VMEM((HIGH * ROWS * 8, 2 * LANES), f32),
            pltpu.VMEM((2, n, 2 * ROWS, HALF), bf16),
            pltpu.VMEM((2, n, 2 * ROWS, HALF), bf16),
            pltpu.VMEM((2, nf, 2 * SG, HALF), bf16),
            pltpu.VMEM((2, SLOTS // 2 * 2 * SG, HALF), bf16),
            pltpu.VMEM((2, n, 2 * ROWS, HALF), bf16),
            pltpu.VMEM((2, n, 2 * ROWS, HALF), bf16),
            pltpu.VMEM((HIGH * ROWS * 8, 2 * LANES), bf16),
            pltpu.VMEM((2, HIGH * ROWS * 8, SIDE), f32),
            dma((n,)), dma((n,)), dma((2, n)), dma((2, n)), dma((2, nf)), dma((2, nf)),
            dma((2, n)), dma((2, n)), dma((8,)),
        ],
        compiler_params=pltpu.CompilerParams(
            collective_id=0, has_side_effects=True, vmem_limit_bytes=62 * 1024 * 1024
        ),
    )(sub_v, sub_u, sub_block, sub_count, gain_real, gain_imag, observed, facets)


def solution(mesh):
    in_specs = (
        P("base", "facet", None, None),
        P("base", None, None),
        P("base"),
        P("base"),
        P("base"),
        P("base"),
        P(),
        P(),
    )
    out_specs = (P("base", "facet", None, None), P("base", None, None))
    return jax.shard_map(
        per_device, mesh=mesh, in_specs=in_specs, out_specs=out_specs, check_vma=False
    )
```

```python
import functools
import math

import jax
import jax.numpy as jnp
from jax import lax
from jax.experimental import pallas as pl
from jax.experimental.pallas import tpu as pltpu
from jax.sharding import PartitionSpec as P

FS = 4096
NPIX = 32768
SG = 32
NF = 16
CMAX = 4096
QUARTER = NPIX // 4
MESH = pl.DeviceIdType.MESH

LOW = 512
SIDE = LOW // 2
HIGH = FS // LOW
COLS = 4
ROWS = 8
SLOTS = 8
LANES = SLOTS * SG
HALF = LANES // 2
STEP = 16


def cos_turns(turns, period=NPIX):
    away = jnp.abs(((turns + period // 2) & (period - 1)) - period // 2)
    x = (period // 4 - away).astype(jnp.float32) * (2.0 * math.pi / period)
    x2 = x * x
    tail = -1.0 / 39916800
    for term in (362880, -5040, 120, -6):
        tail = tail * x2 + 1.0 / term
    return x + x * (x2 * tail)


def iota(shape, dim):
    return lax.broadcasted_iota(jnp.int32, shape, dim)


def per_lane(values, shape):
    owner = iota(shape, len(shape) - 1) // SG
    out = jnp.full(shape, values[0])
    for s in range(1, SLOTS):
        out = jnp.where(owner == s, values[s], out)
    return out


def turned(one, two, c, s):
    return one * c + two * s, two * c - one * s


def phase_plan():
    shape = (64, LANES)
    group = iota(shape, 0) // 8
    line = iota(shape, 0) % 8
    facet = (line // 2 + 2) * 2 * FS + LOW - 1
    shift = jnp.where(line == 0, STEP, jnp.where(line == 1, STEP * STEP, LOW // 2 << line))
    distance = jnp.where(group < 2, 2 * line + 1, jnp.where(group < 4, line * 2 * STEP, facet))
    distance = jnp.where(group < 6, distance, shift)
    sine = (group == 1) | (group == 3) | (group == 7)
    quarter = jnp.where(group == 4, -(line % 2), jnp.where(group == 5, 1 - line % 2, 0))
    return distance, jnp.where(sine, -1, quarter) * 2 * QUARTER


def fill_tables(f, distance, quarter, low, one, two):
    table = cos_turns(jnp.concatenate([f] * 8, 0) * distance[...] + quarter[...], 2 * NPIX)

    def by(i):
        return table[48 + i : 49 + i], table[56 + i : 57 + i]

    def add(pair, turn):
        return pair[0] * turn[0] - pair[1] * turn[1], pair[1] * turn[0] + pair[0] * turn[1]

    fine = (table[0:8], table[8:16])
    more = add(fine, by(0))
    fine = tuple(jnp.concatenate([x, y], 0) for x, y in zip(fine, more))
    steps = [(table[16:24], table[24:32])]
    steps.append(add(steps[0], by(1)))
    lines = [(table[32:40], table[40:48])]
    for i in range(3):
        lines += [turned(*line, *by(2 + i)) for line in lines]
    for h in range(HIGH):
        one[h] = lines[h][0]
        two[h] = lines[h][1]
    for i in range(SIDE // STEP):
        step = tuple(x[i % 8 : i % 8 + 1] for x in steps[i // 8])
        cos, sin = add(fine, step)
        rows = pl.ds(i * STEP, STEP)
        low[rows, 0:LANES] = cos.astype(jnp.bfloat16)
        low[rows, LANES : 2 * LANES] = sin.astype(jnp.bfloat16)


def kernel(
    n, nf, scale,
    v_ref, u_ref, block_ref, count_ref, gain_re_ref, gain_im_ref, seen_cells, facet_ref,
    out_ref, res_ref,
    plus, minus, freq, distance, quarter, low, one, two, row_table,
    product, strip_out, strip, model, blocks, lift, lifted, spread, image,
    v_send, v_recv, s_send, s_recv, m_send, m_recv, l_send, l_recv,
):
    me = lax.axis_index("base")
    mf = lax.axis_index("facet")
    pairs = n // 2

    def device(k, j):
        return {"base": lax.rem(me + k, n), "facet": lax.rem(mf + j, nf)}

    barrier = pltpu.get_barrier_semaphore()

    def greet(k, _):
        pl.semaphore_signal(barrier, inc=1, device_id=device(k, 0), device_id_type=MESH)
        return 0

    lax.fori_loop(1, n, greet, 0)
    for j in range(1, nf):
        pl.semaphore_signal(barrier, inc=1, device_id=device(0, j), device_id_type=MESH)

    freq[me] = per_lane([v_ref[s] for s in range(SLOTS)], (8, LANES)) + iota((8, LANES), 1) % SG
    distance[...], quarter[...] = phase_plan()

    flip = (iota((SIDE, SIDE), 0) + iota((SIDE, SIDE), 1) == SIDE - 1).astype(jnp.float32)
    left = [facet_ref[:, h * LOW : h * LOW + SIDE] for h in range(HIGH)]
    right = [facet_ref[:, h * LOW + SIDE : (h + 1) * LOW] for h in range(HIGH)]
    left = jnp.dot(
        jnp.concatenate(left, 0), flip.astype(jnp.bfloat16), preferred_element_type=jnp.float32
    )
    right = jnp.concatenate(right, 0).astype(jnp.float32)
    plus[...] = (right + left).astype(jnp.bfloat16)
    minus[...] = (right - left).astype(jnp.bfloat16)

    pl.semaphore_wait(barrier, n - 1 + nf - 1)

    def v_copy(k, slot):
        return pltpu.make_async_remote_copy(
            src_ref=freq.at[me], dst_ref=freq.at[slot], send_sem=v_send.at[k],
            recv_sem=v_recv.at[k], device_id=device(k, 0), device_id_type=MESH,
        )

    def send_v(k, _):
        v_copy(k, me).start()
        return 0

    lax.fori_loop(1, n, send_v, 0)

    wide = n * 2 * ROWS
    lane = iota((2 * SG, wide), 1)
    sub = iota((2 * SG, wide), 0)
    turn = (sub // SG - lane // ROWS % 2) * QUARTER
    first = (FS - n * ROWS) // 2 + lane // (2 * ROWS) * ROWS + lane % ROWS

    place = first + (mf + 2) * FS

    def fill_rows(s, _):
        row_table[pl.ds(pl.multiple_of(s * 2 * SG, 2 * SG), 2 * SG), :] = cos_turns(
            (sub % SG + u_ref[s]) * place + turn
        ).astype(jnp.bfloat16)
        return 0

    lax.fori_loop(0, SLOTS, fill_rows, 0)

    def strip_copy(half, k, slot):
        return pltpu.make_async_remote_copy(
            src_ref=strip_out.at[half, k], dst_ref=strip.at[half, slot],
            send_sem=s_send.at[half, k], recv_sem=s_recv.at[half, k], device_id=device(k, 0),
            device_id_type=MESH,
        )

    def model_copy(half, j, slot):
        return pltpu.make_async_remote_copy(
            src_ref=model.at[half, mf], dst_ref=model.at[half, slot],
            send_sem=m_send.at[half, j], recv_sem=m_recv.at[half, j], device_id=device(0, j),
            device_id_type=MESH,
        )

    def lift_copy(half, k, slot):
        return pltpu.make_async_remote_copy(
            src_ref=lift.at[half, lax.rem(me + k, n)], dst_ref=lifted.at[half, slot],
            send_sem=l_send.at[half, k], recv_sem=l_recv.at[half, k], device_id=device(k, 0),
            device_id_type=MESH,
        )

    def take_v(k):
        v_copy(n - k, lax.rem(me + k, n)).wait_recv()

    def degrid(half, i):
        k = 2 * i
        g = lax.rem(me + k, n)
        g_next = lax.rem(me + k + 1, n)
        if half == 0:
            pl.when(k > 0)(lambda: take_v(k))
            take_v(k + 1)
        at = half * pairs + i
        part = slice(half * HALF, (half + 1) * HALF)
        f = jnp.concatenate([freq[g][:, part], freq[g_next][:, part]], 1)
        fill_tables(f, distance, quarter, low.at[at], one.at[at], two.at[at])
        product[:, :LANES] = jnp.dot(
            plus[...], low[at, :, :LANES], preferred_element_type=jnp.float32
        )
        product[:, LANES:] = jnp.dot(
            minus[...], low[at, :, LANES:], preferred_element_type=jnp.float32
        )
        lines_re = []
        lines_im = []
        for r in range(ROWS):
            total_re = jnp.zeros((8, LANES), jnp.float32)
            total_im = jnp.zeros((8, LANES), jnp.float32)
            for h in range(HIGH):
                rows = pl.ds((h * ROWS + r) * 8, 8)
                part_cos = product[rows, 0:LANES]
                part_sin = product[rows, LANES : 2 * LANES]
                total_re = total_re + (part_cos * one[at, h] + part_sin * two[at, h])
                total_im = total_im + (part_cos * two[at, h] - part_sin * one[at, h])
            lines_re.append(jnp.sum(total_re, 0, keepdims=True))
            lines_im.append(jnp.sum(total_im, 0, keepdims=True))
        chunk = jnp.concatenate(lines_re + lines_im, 0).astype(jnp.bfloat16)
        strip_out[half, k] = chunk[:, :HALF]
        strip_out[half, k + 1] = chunk[:, HALF:]

        @pl.when(k == 0)
        def _():
            strip[half, me] = strip_out[half, 0]

        @pl.when(k > 0)
        def _():
            strip_copy(half, k, me).start()

        strip_copy(half, k + 1, me).start()

    half_rows = SLOTS // 2 * 2 * SG
    owner = iota((2 * SG, HALF), 1) // SG

    def sum_rows(half):
        def take(k, _):
            strip_copy(half, k, lax.rem(me + n - k, n)).wait_recv()
            return 0

        lax.fori_loop(1, n, take, 0)
        crossed = jnp.dot(
            row_table[half * half_rows : (half + 1) * half_rows, :],
            strip[half].reshape(wide, HALF),
            preferred_element_type=jnp.float32,
        )
        part = jnp.zeros((2 * SG, HALF), jnp.float32)
        for s in range(SLOTS // 2):
            part = jnp.where(owner == s, crossed[s * 2 * SG : (s + 1) * 2 * SG], part)
        model[half, mf] = (part * scale).astype(jnp.bfloat16)
        for j in range(1, nf):
            model_copy(half, j, mf).start()

    def raise_rows(half):
        full = (SG, LANES)
        part = slice(half * HALF, (half + 1) * HALF)
        gain_re = per_lane([gain_re_ref[block_ref[s]] for s in range(SLOTS)], full)[:, part]
        gain_im = per_lane([gain_im_ref[block_ref[s]] for s in range(SLOTS)], full)[:, part]
        weight = per_lane([count_ref[s] for s in range(SLOTS)], full)[:, part]
        weight = weight.astype(jnp.float32) / CMAX
        seen = seen_cells[:, part].astype(jnp.float32)
        for j in range(1, nf):
            model_copy(half, j, lax.rem(mf + nf - j, nf)).wait_recv()
        whole = model[half, 0].astype(jnp.float32)
        for j in range(1, nf):
            whole = whole + model[half, j].astype(jnp.float32)
        model_re = whole[:SG]
        model_im = whole[SG:]
        diff_re = seen[:SG] - (gain_re * model_re - gain_im * model_im)
        diff_im = seen[SG:] - (gain_re * model_im + gain_im * model_re)
        res_re = weight * (gain_re * diff_re + gain_im * diff_im)
        res_im = weight * (gain_re * diff_im - gain_im * diff_re)
        residual = jnp.concatenate([res_re, res_im], 0)
        res_ref[:, part] = residual.astype(jnp.bfloat16)
        blocks[half] = jnp.concatenate(
            [
                jnp.where(owner == s, residual, 0.0).astype(jnp.bfloat16)
                for s in range(SLOTS // 2)
            ],
            0,
        )
        raised = lax.dot_general(
            row_table[half * half_rows : (half + 1) * half_rows, :],
            blocks[half],
            (((0,), (0,)), ((), ())),
            preferred_element_type=jnp.float32,
        )
        lift[half] = raised.astype(jnp.bfloat16).reshape(n, 2 * ROWS, HALF)

        def send(k, _):
            lift_copy(half, k, me).start()
            return 0

        lax.fori_loop(1, n, send, 0)
        lifted[half, me] = lift[half, me]

    def grid(half, i):
        k = 2 * i
        g = lax.rem(me + k, n)
        g_next = lax.rem(me + k + 1, n)
        pl.when(k > 0)(lambda: lift_copy(half, n - k, g).wait_recv())
        lift_copy(half, n - k - 1, g_next).wait_recv()
        at = half * pairs + i
        value = jnp.concatenate([lifted[half, g], lifted[half, g_next]], 1)
        value = value.astype(jnp.float32) * scale
        for h in range(HIGH):
            for r in range(0, ROWS, 2):
                by_cos = []
                by_sin = []
                for t in (r, r + 1):
                    re = value[t : t + 1]
                    im = value[ROWS + t : ROWS + t + 1]
                    by_cos.append(re * one[at, h] + im * two[at, h])
                    by_sin.append(re * two[at, h] - im * one[at, h])
                rows = pl.ds((h * ROWS + r) * 8, 16)
                spread[rows, 0:LANES] = jnp.concatenate(by_cos, 0).astype(jnp.bfloat16)
                spread[rows, LANES : 2 * LANES] = jnp.concatenate(by_sin, 0).astype(jnp.bfloat16)
        for p in range(2):
            lanes = slice(p * LANES, (p + 1) * LANES)
            image[p] += lax.dot_general(
                spread[:, lanes],
                low[at, :, lanes],
                (((1,), (1,)), ((), ())),
                preferred_element_type=jnp.float32,
            )

    def loop(first, last, step, half):
        def body(i, _):
            step(half, i)
            return 0

        lax.fori_loop(first, last, body, 0)

    middle = (pairs + 1) // 2
    loop(0, pairs, degrid, 0)
    loop(0, middle, degrid, 1)
    sum_rows(0)
    loop(middle, pairs, degrid, 1)
    raise_rows(0)
    sum_rows(1)
    image[...] = jnp.zeros(image.shape, jnp.float32)
    loop(0, middle, grid, 0)
    raise_rows(1)
    loop(middle, pairs, grid, 0)

    loop(0, pairs, grid, 1)
    right = image[0] + image[1]
    left = jnp.dot(
        image[0] - image[1],
        flip,
        preferred_element_type=jnp.float32,
        precision=lax.Precision.HIGHEST,
    )
    for h in range(HIGH):
        rows = slice(h * 8 * ROWS, (h + 1) * 8 * ROWS)
        both = jnp.concatenate([left[rows], right[rows]], 1)
        out_ref[:, h * LOW : (h + 1) * LOW] = both

    def drain(k, _):
        v_copy(k, me).wait_send()
        for half in range(2):
            strip_copy(half, k, me).wait_send()
            lift_copy(half, k, me).wait_send()
        return 0

    lax.fori_loop(1, n, drain, 0)
    for half in range(2):
        for j in range(1, nf):
            model_copy(half, j, mf).wait_send()


def per_device(facets, observed, sub_u, sub_v, sub_block, sub_count, gain_real, gain_imag):
    n = lax.axis_size("base")
    nf = lax.axis_size("facet")
    assert facets.shape == (ROWS, COLS, 2, FS) and nf * COLS == NF and n % 2 == 0
    assert observed.shape == (SLOTS, 2, SG * SG)
    scale = 1.0 / math.sqrt(NF * n * ROWS * FS)
    rows = facets.reshape(ROWS * COLS * 2, FS)
    seen = observed.reshape(SLOTS, 2, SG, SG).transpose(1, 2, 0, 3).reshape(2 * SG, LANES)
    smem = pl.BlockSpec(memory_space=pltpu.SMEM)
    vmem = pl.BlockSpec(memory_space=pltpu.VMEM)
    bf16 = jnp.bfloat16
    f32 = jnp.float32
    dma = pltpu.SemaphoreType.DMA
    out, res = pl.pallas_call(
        functools.partial(kernel, n, nf, scale),
        out_shape=(
            jax.ShapeDtypeStruct((ROWS * COLS * 2, FS), f32),
            jax.ShapeDtypeStruct((2 * SG, LANES), bf16),
        ),
        in_specs=[smem] * 6 + [vmem] * 2,
        out_specs=(vmem, vmem),
        scratch_shapes=[
            pltpu.VMEM((HIGH * ROWS * 8, SIDE), bf16),
            pltpu.VMEM((HIGH * ROWS * 8, SIDE), bf16),
            pltpu.VMEM((n, 8, LANES), jnp.int32),
            pltpu.VMEM((64, LANES), jnp.int32),
            pltpu.VMEM((64, LANES), jnp.int32),
            pltpu.VMEM((n, SIDE, 2 * LANES), bf16),
            pltpu.VMEM((n, HIGH, 8, LANES), f32),
            pltpu.VMEM((n, HIGH, 8, LANES), f32),
            pltpu.VMEM((SLOTS * 2 * SG, n * 2 * ROWS), bf16),
            pltpu.VMEM((HIGH * ROWS * 8, 2 * LANES), f32),
            pltpu.VMEM((2, n, 2 * ROWS, HALF), bf16),
            pltpu.VMEM((2, n, 2 * ROWS, HALF), bf16),
            pltpu.VMEM((2, nf, 2 * SG, HALF), bf16),
            pltpu.VMEM((2, SLOTS // 2 * 2 * SG, HALF), bf16),
            pltpu.VMEM((2, n, 2 * ROWS, HALF), bf16),
            pltpu.VMEM((2, n, 2 * ROWS, HALF), bf16),
            pltpu.VMEM((HIGH * ROWS * 8, 2 * LANES), bf16),
            pltpu.VMEM((2, HIGH * ROWS * 8, SIDE), f32),
            dma((n,)), dma((n,)), dma((2, n)), dma((2, n)), dma((2, nf)), dma((2, nf)),
            dma((2, n)), dma((2, n)),
        ],
        compiler_params=pltpu.CompilerParams(
            collective_id=0, has_side_effects=True, vmem_limit_bytes=48 * 1024 * 1024
        ),
    )(sub_v, sub_u, sub_block, sub_count, gain_real, gain_imag, seen, rows)
    res = res.reshape(2, SG, SLOTS, SG).transpose(2, 0, 1, 3)
    return (out.reshape(ROWS, COLS, 2, FS), res.reshape(SLOTS, 2, SG * SG))


def solution(mesh):
    in_specs = (
        P("base", "facet", None, None),
        P("base", None, None),
        P("base"),
        P("base"),
        P("base"),
        P("base"),
        P(),
        P(),
    )
    out_specs = (P("base", "facet", None, None), P("base", None, None))
    return jax.shard_map(
        per_device, mesh=mesh, in_specs=in_specs, out_specs=out_specs, check_vma=False
    )
```
